256 devices in a mesh: vis: 64 (over z, x, core), head: 4 (over y).
Axes of the slice: x: 4, y: 4, z: 8, core: 2. Of those that a mesh axis runs over, the one named last changes fastest.
Arguments:
- patches: bfloat16 [24576, 1280], P('vis'), may hold values from -6 to 6
- norm_gain: float32 [1280], replicated, may hold values from 0.4 to 1.6
- w_qkv: bfloat16 [1280, 3, 1280], P(None, None, 'head'), may hold values from -1 to 1
- w_out: bfloat16 [1280, 1280], P(None, 'head'), may hold values from -0.15625 to 0.15625
- grad_y: bfloat16 [24576, 1280], P('vis'), may hold values from -16 to 16
- window_ids: int32 [24576], replicated, may hold values from 0 to 511, never falling along the last dimension, each value on 1 to 64 neighbouring positions
Outputs:
- grad_x: bfloat16 [24576, 1280], P('vis', 'head')
- grad_qkv: float32 [1280, 3, 1280], P('vis', None, 'head')
- grad_out: float32 [1280, 1280], P('vis', 'head')
- grad_gain: float32 [1280], P('head')
The draws below stay inside these ranges and needn't reach their ends.
Inputs may be any that keep to these rules, and one draw needn't show every extreme that they name: `window_ids`: window numbers never fall along the patches, and each window holds 1 to 64 patches, one exactly 64.
All inputs are finite; a program needn't handle non-finite values.
Results may differ from the reference program's by a relative error of at most 0.03.
Values may be sent and summed in bfloat16 or wider, within the bound.
A program may use at most 64 MiB of HBM per device.

```python
import math
import jax
import jax.numpy as jnp
import numpy as np
from jax import lax

D = 1280
HEAD_DIM = 80
WIN = 64
ROWS_DEV = 384
ROWS = 24576
WINDOWS = 512


def draw_patches(key, part):
    key = jax.random.fold_in(key, 11)
    noise_key = jax.random.fold_in(key, 0)
    values = jnp.clip(jax.random.normal(noise_key, (ROWS, D), jnp.float32), -6.0, 6.0)
    return values.astype(jnp.bfloat16)


def draw_w_qkv(key, part):
    key = jax.random.fold_in(key, 23)
    base_key = jax.random.fold_in(key, 0)
    values = jnp.clip(jax.random.normal(base_key, (D, 3, D), jnp.float32), -6.0, 6.0) * D ** (-0.5)
    return values.astype(jnp.bfloat16)


def with_spikes(array, own_key, source, target, shards_of, factor):
    def block_of(axis_at):
        return (jnp.arange(array.shape[axis_at]) // (array.shape[axis_at] // shards_of)).reshape((-1,) + (1,) * (array.ndim - 1 - axis_at))

    first = jax.random.permutation(own_key, shards_of)[block_of(target)]
    other_side = (block_of(target) + shards_of // 2) % shards_of
    return jnp.where((block_of(source) == first) | (block_of(source) == other_side), factor * array, array)


def shard_levels(key, dims, shards, low, largest):
    gain = 1.0
    for axis_at, blocks in shards:
        draws = jax.random.uniform(jax.random.fold_in(jax.random.fold_in(key, 6), axis_at), (blocks,), jnp.float32, low / len(shards), largest / len(shards))
        gain = gain * jnp.repeat(jnp.exp(draws), dims[axis_at] // blocks).reshape((-1,) + (1,) * (len(dims) - 1 - axis_at))
    return gain


def length_profile(amount, total, bound, slope):
    weights = [(1 << 20) // math.isqrt(rank ** slope) + 1 for rank in range(2, amount + 1)]
    rest, counts = total - bound - (amount - 1), [1] * (amount - 1)
    while rest > 0:
        free = [i for i in range(amount - 1) if counts[i] < bound]
        mass, budget = sum([weights[i] for i in free]), rest
        for i in free:
            extra = min(bound - counts[i], max(1, budget * weights[i] // mass), rest)
            counts[i] = counts[i] + extra
            rest = rest - extra
    return np.array([bound] + counts)


def uneven(rng, amount, total, bound, skew):
    if amount == 2:
        one = jax.random.randint(rng, (), max(1, total - bound), min(bound, total - 1) + 1)
        return jnp.stack([one, total - one])
    sizes = jnp.asarray(length_profile(amount, total, bound, skew), jnp.int32)
    twos = (amount - 1) // 2
    donor, sink = sizes[1:1 + 2 * twos:2], sizes[2:2 + 2 * twos:2]
    slack = jnp.minimum(donor - 1, bound - sink)
    shifted = jax.random.randint(jax.random.fold_in(rng, 1), (twos,), 0, 1 << 20) % (slack + 1)
    sizes = sizes.at[1:1 + 2 * twos:2].set(donor - shifted).at[2:2 + 2 * twos:2].set(sink + shifted)
    return sizes[jax.random.permutation(jax.random.fold_in(rng, 2), amount)]


def bell_draw(key, shape, deviation, reach, cuts=(), held_as=jnp.bfloat16):
    factor_of = shard_levels(key, shape, cuts, -0.22, 0.18) if cuts else 1.0
    entries = jax.random.normal(key, shape, jnp.float32) * deviation * factor_of
    return jnp.minimum(jnp.maximum(entries, -reach), reach).astype(held_as)


def gaussian_with(rng, dims, width, most, cuts, heavy, kind=jnp.bfloat16):
    values = width * jax.random.normal(rng, dims, jnp.float32)
    if cuts:
        values = values * shard_levels(rng, dims, cuts, -0.22, 0.18)
    return jnp.clip(with_spikes(values, jax.random.fold_in(rng, 3), *heavy), -most, most).astype(kind)


def setup_inputs(seed: int = 0) -> dict:
    seeds = jax.random.split(jax.random.key(seed), 7)
    return {
        "patches": draw_patches(jax.random.fold_in(seeds[6], 71), 0),
        "norm_gain": jnp.clip(1.0 + 0.12 * jax.random.normal(seeds[1], (D,), jnp.float32), 0.4, 1.6),
        "w_qkv": draw_w_qkv(jax.random.fold_in(seeds[6], 71), 0),
        "w_out": bell_draw(seeds[3], (D, D), D ** -0.5, 0.15625, ((1, 4),)),
        "grad_y": gaussian_with(seeds[4], (ROWS, D), 1.0, 16.0, ((0, 64),), (0, 1, 64, 4.0)),
        "window_ids": jnp.searchsorted(jnp.cumsum(uneven(seeds[5], WINDOWS, ROWS, WIN, 0)), jnp.arange(ROWS), side="right").astype(jnp.int32),
    }


norm_epsilon = 1e-06

def attention_grads(query, keyval, own_ids, key_ids, grad_att):
    f32 = jnp.float32
    row_count = query.shape[0]
    key_span = keyval.shape[0]
    heads = query.shape[1] // HEAD_DIM
    scale = HEAD_DIM ** (-0.5)
    q_heads = query.reshape(row_count, heads, HEAD_DIM).astype(f32)
    k_heads = keyval[:, 0].reshape(key_span, heads, HEAD_DIM).astype(f32)
    v_heads = keyval[:, 1].reshape(key_span, heads, HEAD_DIM).astype(f32)
    g_heads = grad_att.reshape(row_count, heads, HEAD_DIM).astype(f32)
    scores = jnp.einsum('rhe,khe->hrk', q_heads, k_heads) * scale
    same_window = own_ids[:, None] == key_ids[None, :]
    scores = jnp.where(same_window[None], scores, -1e+30)
    highest = lax.optimization_barrier(jnp.max(scores, axis=2, keepdims=True))
    weights = jnp.exp(scores - highest)
    weights = weights / lax.optimization_barrier(jnp.sum(weights, axis=2, keepdims=True))
    probs = weights.astype(jnp.bfloat16)
    attended = jnp.einsum('hrk,khe->rhe', probs.astype(f32), v_heads).astype(jnp.bfloat16)
    delta = lax.optimization_barrier(jnp.sum(attended.astype(f32) * g_heads, axis=2))
    dprob = jnp.einsum('rhe,khe->hrk', g_heads, v_heads)
    dscore = (weights * (dprob - jnp.transpose(delta)[:, :, None]) * scale).astype(jnp.bfloat16)
    grad_q = jnp.einsum('hrk,khe->rhe', dscore.astype(f32), k_heads).astype(jnp.bfloat16)
    grad_k = jnp.einsum('hrk,rhe->khe', dscore.astype(f32), q_heads)
    grad_v = jnp.einsum('hrk,rhe->khe', probs.astype(f32), g_heads)
    key_grads = jnp.stack([grad_k.reshape(key_span, -1), grad_v.reshape(key_span, -1)], axis=1)
    return (attended.reshape(row_count, -1), grad_q.reshape(row_count, -1), key_grads)

def reference(patches, norm_gain, w_qkv, w_out, grad_y, window_ids):
    f32 = jnp.float32
    bf16 = jnp.bfloat16
    inputs = patches.astype(f32)
    inverse = lax.rsqrt(lax.optimization_barrier(jnp.mean(inputs * inputs, axis=1, keepdims=True)) + norm_epsilon)
    normed = (inputs * inverse * norm_gain[None, :]).astype(bf16)
    project = jnp.einsum('rd,dcj->rcj', normed.astype(f32), w_qkv.astype(f32)).astype(bf16)
    grad_att = jnp.dot(grad_y, w_out, preferred_element_type=f32).astype(bf16)
    blocks = ROWS // ROWS_DEV
    key_span = ROWS_DEV + 2 * WIN
    padded = jnp.pad(project[:, 1:], ((WIN, WIN), (0, 0), (0, 0)))
    padded_ids = jnp.pad(window_ids, (WIN, WIN), constant_values=-1)
    queries = project[:, 0]

    def one_block(block):
        start = (block * ROWS_DEV).astype(jnp.int32)
        query = lax.dynamic_slice_in_dim(queries, start, ROWS_DEV, 0)
        keyval = lax.dynamic_slice_in_dim(padded, start, key_span, 0)
        own_ids = lax.dynamic_slice_in_dim(window_ids, start, ROWS_DEV, 0)
        key_ids = lax.dynamic_slice_in_dim(padded_ids, start, key_span, 0)
        grad_rows = lax.dynamic_slice_in_dim(grad_att, start, ROWS_DEV, 0)
        return attention_grads(query, keyval, own_ids, key_ids, grad_rows)
    attended, grad_q, key_grads = lax.map(one_block, jnp.arange(blocks, dtype=jnp.int32))
    center = key_grads[:, WIN:WIN + ROWS_DEV]
    upper_rim = key_grads[:, :WIN]
    lower_rim = key_grads[:, WIN + ROWS_DEV:]
    zero_rim = jnp.zeros_like(upper_rim[:1])
    center = center.at[:, ROWS_DEV - WIN:].add(jnp.concatenate([upper_rim[1:], zero_rim], axis=0))
    center = center.at[:, :WIN].add(jnp.concatenate([zero_rim, lower_rim[:-1]], axis=0))
    grad_kv = center.reshape(ROWS, 2, D).astype(bf16)
    attended = attended.reshape(ROWS, D)
    grad_proj = jnp.concatenate([grad_q.reshape(ROWS, 1, D), grad_kv], axis=1)
    grad_normed = jnp.einsum('rcj,dcj->rd', grad_proj.astype(f32), w_qkv.astype(f32))
    grad_qkv = jnp.einsum('rd,rcj->dcj', normed.astype(f32), grad_proj.astype(f32))
    grad_out = jnp.einsum('ro,ri->oi', grad_y.astype(f32), attended.astype(f32))
    grad_gain = lax.optimization_barrier(jnp.sum(grad_normed * inputs * inverse, axis=0))
    scaled = grad_normed * norm_gain[None, :]
    product_mean = lax.optimization_barrier(jnp.mean(scaled * inputs, axis=1, keepdims=True))
    grad_x = (grad_y.astype(f32) + inverse * (scaled - inputs * inverse * inverse * product_mean)).astype(bf16)
    return (grad_x, grad_qkv, grad_out, grad_gain)
```

```python
import functools

import jax
import jax.numpy as jnp
from jax import lax
from jax.experimental import pallas as pl
from jax.experimental.pallas import tpu as pltpu
from jax.sharding import PartitionSpec as P

f32 = jnp.float32
bf16 = jnp.bfloat16
D = 1280
HD = 80
R = 384
SCALE = HD ** (-0.5)
EPS = 1e-06
MESH = pl.DeviceIdType.MESH
NEG = -1e30
WIDTHS = (256, 384)


def nn(a, b):
    return lax.dot_general(a, b, (((1,), (0,)), ((), ())), preferred_element_type=f32)


def nt(a, b, precision=None):
    return lax.dot_general(
        a, b, (((1,), (1,)), ((), ())), preferred_element_type=f32, precision=precision
    )


NAMES = ["proj", "halo0", "halo1", "nt", "gyt", "gt0", "gt1", "core", "gcore"]
NAMES += [f"r{s}{t}" for s in range(2) for t in range(4)]
NAMES += [f"l{s}{t}" for s in range(2) for t in range(4)]
NAMES += [f"x{s}{d}" for s in range(2) for d in range(1, 4)]
NAMES += [f"y{d}" for d in range(1, 4)] + [f"s{d}" for d in range(1, 4)]
NAMES += [f"gx{d}" for d in range(1, 4)] + [f"gz{d}" for d in range(1, 8)]
MSG = {name: i for i, name in enumerate(NAMES)}


def kernel(
    x_hbm, gy_hbm, wt_hbm, wo_hbm, ids_hbm, gain_hbm,
    gx_out, gqkv_out, gout_out, ggain_out,
    x_v, gy_v, wt, wo, ids, gain,
    xt, nrm, gyt, wn, gcol, inv,
    psend, proj, halo, kn, vn, idr, idc, main, sec,
    gt, at, gtr,
    p0, p1, r0, r1, l0, l1, r0h, r1h, l0h, l1h,
    a0, a1, xs0, xs1, xr0, xr1, csend, crecv,
    gnf, ysend, yrecv, ssend, srecv,
    gxs, gxr, gcs, gcr, gzs, gzr,
    lsem, send_sem, recv_sem,
):
    v = lax.axis_index("vis")
    h = lax.axis_index("head")
    c = lax.rem(v, 2)
    q = v // 2
    x = lax.rem(q, 4)
    z = v // 8
    dev = lambda zz, xx, cc: (zz * 8 + xx * 2 + cc, h)
    zdev = lambda d: dev(lax.rem(z + d + 8, 8), x, c)
    xdev = lambda d: dev(z, lax.rem(x + d, 4), c)
    ydev = lambda d: (v, lax.rem(h + d, 4))
    peer = (v + 1 - 2 * c, h)
    chip = lambda d, cc: (2 * lax.rem(q + d + 32, 32) + cc, h)

    loads = []

    def load(src, dst):
        cp = pltpu.make_async_copy(src, dst, lsem.at[len(loads)])
        cp.start()
        loads.append(cp)
        return cp

    ld_x = load(x_hbm, x_v)
    ld_gain = load(gain_hbm, gain)
    ld_gy = load(gy_hbm, gy_v)
    ld_w = []
    for k in (2, 3, 0, 1):
        half = c if k < 2 else 1 - c
        for comp in range(3):
            src = pl.multiple_of(320 * comp + 160 * half + 80 * (k % 2), 16)
            ld_w.append(load(wt_hbm.at[pl.ds(src, 80), :], wt.at[pl.ds(240 * k + 80 * comp, 80), :]))
    for k in (1, 0):
        half = c if k == 0 else 1 - c
        src = pl.multiple_of(160 * half, 16)
        ld_w.append(load(wo_hbm.at[pl.ds(src, 160), :], wo.at[pl.ds(160 * k, 160), :]))
    ld_ids = load(ids_hbm, ids)

    barrier = pltpu.get_barrier_semaphore()
    greet = [peer]
    greet += [zdev(d) for d in range(1, 8)]
    greet += [xdev(d) for d in range(1, 4)]
    greet += [ydev(d) for d in range(1, 4)]
    greet += [chip(2 * c - 1, 0), chip(2 * c - 1, 1), chip(1 - 2 * c, c)]
    for d in greet:
        pl.semaphore_signal(barrier, inc=1, device_id=d, device_id_type=MESH)

    copies = {}

    def send(name, src, dst, to):
        i = MSG[name]
        cp = pltpu.make_async_remote_copy(
            src_ref=src, dst_ref=dst, send_sem=send_sem.at[i], recv_sem=recv_sem.at[i],
            device_id=to, device_id_type=MESH,
        )
        cp.start()
        copies[name] = cp

    def arrived(name):
        copies[name].wait_recv()

    ld_x.wait()
    ld_gain.wait()
    xt[...] = x_v[...].T
    for i in range(10):
        gcol[pl.ds(128 * i, 128), :] = jnp.broadcast_to(gain[pl.ds(i, 1), :], (128, 128)).T
    for b in range(3):
        lanes = pl.ds(128 * b, 128)
        xf = xt[:, lanes].astype(f32)
        iv = lax.rsqrt(jnp.sum(xf * xf, axis=0, keepdims=True) * (1.0 / D) + EPS)
        inv[:, lanes] = iv
        nrm[:, lanes] = (xf * iv * gcol[...]).astype(bf16)
    ld_gy.wait()
    gyt[:, 0:R] = gy_v[...].T
    for cp in ld_w:
        cp.wait()
    ld_ids.wait()

    def project(half, dst):
        pa = nn(wt[pl.ds(480 * half, 480), :], nrm[:, 0:R]).astype(bf16)
        pg = nn(wo[pl.ds(160 * half, 160), :], gyt[:, 0:R]).astype(bf16)
        for b in range(3):
            dst[b, 0:480, :] = pa[:, 128 * b : 128 * b + 128]
            dst[b, 480:640, :] = pg[:, 128 * b : 128 * b + 128]

    project(1, psend)
    pl.semaphore_wait(barrier, len(greet))
    edge = 2 * c
    send("halo1", psend.at[edge], halo.at[c], chip(2 * c - 1, 1 - c))
    send("proj", psend, proj.at[pl.ds(3, 3)], peer)
    project(0, proj)
    send("halo0", proj.at[edge], halo.at[c], chip(2 * c - 1, c))
    send("gyt", gyt.at[:, pl.ds(0, R)], gyt.at[:, pl.ds(R, R)], peer)
    send("nt", nrm.at[:, pl.ds(0, R)], nrm.at[:, pl.ds(R, R)], peer)

    for s in range(3):
        idr[pl.ds(s, 1), :] = ids[pl.ds(6 * q + 3 * c + s, 1), :]
        idr[pl.ds(3 + s, 1), :] = ids[pl.ds(6 * q + 3 - 3 * c + s, 1), :]
    lane1 = lax.broadcasted_iota(jnp.int32, (1, 128), 1) < 64
    after = ids[pl.ds(lax.rem(6 * q + 6, 192), 1), :]
    before = ids[pl.ds(lax.rem(6 * q + 191, 192), 1), :]
    idr[pl.ds(6, 1), :] = jnp.where(lane1, after, before)
    for s in range(7):
        idc[s] = jnp.broadcast_to(idr[pl.ds(s, 1), :], (128, 128)).T

    wn[...] = wt[...].T

    def natural(s):
        for k in range(2):
            kn[2 * s + k] = proj[s, pl.ds(240 * k + 80, 80), :].T
            vn[2 * s + k] = proj[s, pl.ds(240 * k + 160, 80), :].T

    for s in range(3):
        natural(s)
    arrived("proj")
    for s in range(3, 6):
        natural(s)
    arrived("halo0")
    arrived("halo1")
    lane = lax.broadcasted_iota(jnp.int32, (640, 128), 1) < 64
    proj[6] = jnp.where(lane, halo[0].astype(f32), halo[1].astype(f32)).astype(bf16)
    natural(6)

    pick = lambda a, b: jnp.where(c == 0, a, b) if a != b else a
    nxt = [pick(*p) for p in ((1, 1), (2, 2), (3, 6), (4, 4), (5, 5), (6, 0), (0, 3))]
    prv = [pick(*p) for p in ((6, 5), (0, 0), (1, 1), (2, 6), (3, 3), (4, 4), (5, 2))]
    lane80 = lax.broadcasted_iota(jnp.int32, (HD, 128), 1) < 64

    def mixed(a, b):
        return jnp.where(lane80, a.astype(f32), b.astype(f32)).astype(bf16)

    def attend(k, s):
        o = 240 * k
        n, p = nxt[s], prv[s]
        qt = proj[s, pl.ds(o, 80), :]
        gq = proj[s, pl.ds(480 + 80 * k, 80), :]
        kt, vt = [
            jnp.concatenate(
                [
                    proj[s, pl.ds(o + w, 80), :],
                    mixed(proj[n, pl.ds(o + w, 80), :], proj[p, pl.ds(o + w, 80), :]),
                ],
                axis=1,
            )
            for w in (80, 160)
        ]
        kk, vv = [
            jnp.concatenate([t[2 * s + k], t[2 * n + k, 0:64], t[2 * p + k, 64:128]], axis=0)
            for t in (kn, vn)
        ]
        key_ids = jnp.concatenate([idc[s], idc[n, 0:64], idc[p, 64:128]], axis=0)
        same = key_ids == idr[pl.ds(s, 1), :]
        scores = jnp.where(same, nn(kk, qt) * SCALE, NEG)
        e = jnp.exp(scores - jnp.max(scores, axis=0, keepdims=True))
        w = e * (1.0 / jnp.sum(e, axis=0, keepdims=True))
        probs = w.astype(bf16)
        att = nn(vt, probs).astype(bf16)
        delta = jnp.sum(att.astype(f32) * gq.astype(f32), axis=0, keepdims=True)
        ds = (w * (nn(vv, gq) - delta) * SCALE).astype(bf16)
        if s < 6:
            at[pl.ds(80 * k, 80), pl.ds(128 * s, 128)] = att
            gt[pl.ds(o, 80), pl.ds(128 * s, 128)] = nn(kt, ds).astype(bf16)
        gk = nt(qt, ds)
        gv = nt(gq, probs)
        main[s, 0:80, :] = gk[:, 0:128]
        main[s, 80:160, :] = gv[:, 0:128]
        sec[s, 0:80, :] = gk[:, 128:256]
        sec[s, 80:160, :] = gv[:, 128:256]

    lane160 = lax.broadcasted_iota(jnp.int32, (2 * HD, 128), 1) < 64

    def head(k):
        for s in range(7):
            attend(k, s)
        for s in range(6):
            total = main[s] + jnp.where(lane160, sec[prv[s]], sec[nxt[s]])
            gt[pl.ds(240 * k + 80, 160), pl.ds(128 * s, 128)] = total.astype(bf16)
        send(f"gt{k}", gt.at[pl.ds(240 * k, 240), pl.ds(R, R)], gtr.at[pl.ds(240 * k, 240), :], peer)

    part, rr, ll = (p0, p1), ((r0h, r0), (r1h, r1)), ((l0h, l0), (l1h, l1))

    def weights(k):
        a = nt(nrm[...], gt[pl.ds(240 * k, 240), :]).astype(bf16)
        b = nt(gyt[...], at[pl.ds(80 * k, 80), :]).astype(bf16)
        for i in range(8):
            rows = slice(160 * i, 160 * i + 160)
            if k == 0:
                p0[i, :, 0:240] = a[rows]
                p0[i, :, 240:256] = b[rows, 0:16]
                p1[i, :, 0:64] = b[rows, 16:80]
            else:
                p1[i, :, 64:304] = a[rows]
                p1[i, :, 304:384] = b[rows]

    def ring_send(s, t):
        if t == 0:
            far = lax.rem(z + 4, 8)
            send(f"r{s}0", part[s].at[far, pl.ds(0, 80)], rr[s][0], zdev(1))
            send(f"l{s}0", part[s].at[far, pl.ds(80, 80)], ll[s][0], zdev(-1))
        else:
            send(f"r{s}{t}", part[s].at[lax.rem(z + 4 - t, 8)], rr[s][1].at[t - 1], zdev(1))
            send(f"l{s}{t}", part[s].at[lax.rem(z + 4 + t, 8)], ll[s][1].at[t - 1], zdev(-1))

    def ring_add(s, t):
        for way, got, at_ in (("r", rr[s], z + 3 - t), ("l", ll[s], z + 5 + t)):
            arrived(f"{way}{s}{t}")
            i = lax.rem(at_, 8)
            if t == 0:
                rows = pl.ds(0, 80) if way == "r" else pl.ds(80, 80)
                total = part[s][i, rows].astype(f32) + got[0][...].astype(f32)
                part[s][i, rows] = total.astype(bf16)
            else:
                total = part[s][i].astype(f32) + got[1][t - 1].astype(f32)
                part[s][i] = total.astype(bf16)
        ring_send(s, t + 1)

    acc, xs, xr = (a0, a1), (xs0, xs1), (xr0, xr1)

    def ring_end(s):
        arrived(f"r{s}3")
        arrived(f"l{s}3")
        total = part[s][z].astype(f32) + rr[s][1][2].astype(f32) + ll[s][1][2].astype(f32)
        for i in range(4):
            piece = total[40 * i : 40 * i + 40]
            acc[s][i] = piece
            xs[s][i] = jnp.concatenate([piece, jnp.zeros((8, WIDTHS[s]), f32)], axis=0).astype(bf16)
        for d in range(1, 4):
            send(f"x{s}{d}", xs[s].at[lax.rem(x + d, 4)], xr[s].at[d - 1], xdev(d))

    def x_end(s):
        total = acc[s][x]
        for d in range(1, 4):
            arrived(f"x{s}{d}")
            total = total + xr[s][d - 1].astype(f32)[0:40]
        return total

    head(0)
    arrived("gyt")
    arrived("nt")
    weights(0)
    ring_send(0, 0)
    head(1)
    weights(1)
    ring_send(1, 0)
    ring_add(0, 0)

    arrived("gt0")
    arrived("gt1")
    ssum = jnp.zeros((1, R), f32)
    for d in (1, 2, 3, 0):
        to = lax.rem(h + d, 4)
        rows = pl.ds(pl.multiple_of(320 * to, 64), 320)
        g = nn(wn[rows, 0:480], gt[:, 0:R]) + nn(wn[rows, 480:960], gtr[...])
        parts = []
        for b in range(3):
            gb = g[:, 128 * b : 128 * b + 128] * gcol[rows, :]
            xb = xt[rows, pl.ds(128 * b, 128)].astype(f32)
            parts.append(jnp.sum(gb * xb, axis=0, keepdims=True))
        ssum = ssum + jnp.concatenate(parts, axis=1)
        if d:
            ysend[d - 1] = g.astype(bf16)
            send(f"y{d}", ysend.at[d - 1], yrecv.at[d - 1], ydev(d))
        else:
            gnf[...] = g
        if d == 1:
            ring_add(1, 0)
        if d == 3:
            ring_add(0, 1)
    ssend[...] = jnp.broadcast_to(ssum, (8, R))
    for d in range(1, 4):
        send(f"s{d}", ssend, srecv.at[d - 1], ydev(d))
    ring_add(1, 1)
    ring_add(0, 2)
    ring_add(1, 2)
    ring_end(0)

    mine = pl.ds(pl.multiple_of(320 * h, 64), 320)
    gn = gnf[...]
    sums = ssum
    for d in range(1, 4):
        arrived(f"y{d}")
        arrived(f"s{d}")
        gn = gn + yrecv[d - 1].astype(f32)
        sums = sums + srecv[d - 1, 0:1, :]
    iv = inv[...]
    xo = xt[mine, :].astype(f32)
    gc = jnp.concatenate([gcol[mine, :]] * 3, axis=1)
    xi = xo * iv
    gx = gyt[mine, 0:R].astype(f32) + iv * (gn * gc - xi * (iv * (sums * (1.0 / D))))
    gx_out[...] = gx.astype(bf16)
    gxs[...] = nt(jnp.ones((8, R), f32), gn * xi, precision=lax.Precision.HIGHEST)
    for d in range(1, 4):
        send(f"gx{d}", gxs, gxr.at[d - 1], xdev(d))

    ring_end(1)
    total = gxs[...]
    for d in range(1, 4):
        arrived(f"gx{d}")
        total = total + gxr[d - 1]
    gcs[...] = total
    send("gcore", gcs, gcr, peer)
    f0 = x_end(0)
    arrived("gcore")
    gzs[...] = gcs[...] + gcr[...]
    for d in range(1, 8):
        send(f"gz{d}", gzs, gzr.at[d - 1], zdev(d))
    f1 = x_end(1)

    both = jnp.concatenate([f0, f1], axis=1)
    low, high = both[0:20], both[20:40]
    first = c == 0
    csend[0:20, :] = jnp.where(first, high, low)
    csend[20:24, :] = jnp.zeros((4, 640), f32)
    send("core", csend, crecv, peer)
    own = jnp.where(first, low, high)
    total = gzs[...]
    for d in range(1, 8):
        arrived(f"gz{d}")
        total = total + gzr[d - 1]
    ggain_out[...] = total[0:1]
    arrived("core")
    other = crecv[0:20, :]
    sides = (jnp.where(first, own, other), jnp.where(first, other, own))
    for i, side in enumerate(sides):
        for k in range(2):
            col = 80 * (2 * i + k)
            for comp in range(3):
                gqkv_out[comp, :, col : col + 80] = side[:, 320 * k + 80 * comp : 320 * k + 80 * comp + 80]
            gout_out[:, col : col + 80] = side[:, 320 * k + 240 : 320 * k + 320]
    for cp in copies.values():
        cp.wait_send()


def per_device(patches, norm_gain, w_qkv, w_out, grad_y, window_ids):
    wt = jnp.transpose(w_qkv, (1, 2, 0)).reshape(960, D)
    wo = jnp.transpose(w_out)
    V = pltpu.VMEM
    w0, w1 = WIDTHS
    scratch = [
        V((R, D), bf16), V((R, D), bf16), V((960, D), bf16), V((320, D), bf16),
        V((192, 128), jnp.int32), V((10, 128), f32),
        V((D, R), bf16), V((D, 2 * R), bf16), V((D, 2 * R), bf16), V((D, 960), bf16),
        V((D, 128), f32), V((1, R), f32),
        V((3, 640, 128), bf16), V((7, 640, 128), bf16), V((2, 640, 128), bf16),
        V((14, 128, HD), bf16), V((14, 128, HD), bf16),
        V((8, 128), jnp.int32), V((7, 128, 128), jnp.int32),
        V((7, 160, 128), f32), V((7, 160, 128), f32),
        V((480, 2 * R), bf16), V((160, 2 * R), bf16), V((480, R), bf16),
        V((8, 160, w0), bf16), V((8, 160, w1), bf16),
        V((3, 160, w0), bf16), V((3, 160, w1), bf16),
        V((3, 160, w0), bf16), V((3, 160, w1), bf16),
        V((80, w0), bf16), V((80, w1), bf16), V((80, w0), bf16), V((80, w1), bf16),
        V((4, 40, w0), f32), V((4, 40, w1), f32),
        V((4, 48, w0), bf16), V((4, 48, w1), bf16),
        V((3, 48, w0), bf16), V((3, 48, w1), bf16),
        V((24, 640), f32), V((24, 640), f32),
        V((320, R), f32), V((3, 320, R), bf16), V((3, 320, R), bf16),
        V((8, R), f32), V((3, 8, R), f32),
        V((8, 320), f32), V((3, 8, 320), f32), V((8, 320), f32), V((8, 320), f32),
        V((8, 320), f32), V((7, 8, 320), f32),
        pltpu.SemaphoreType.DMA((18,)),
        pltpu.SemaphoreType.DMA((len(NAMES),)),
        pltpu.SemaphoreType.DMA((len(NAMES),)),
    ]
    gx, gqkv, gout, ggain = pl.pallas_call(
        kernel,
        out_shape=(
            jax.ShapeDtypeStruct((320, R), bf16),
            jax.ShapeDtypeStruct((3, 20, 320), f32),
            jax.ShapeDtypeStruct((20, 320), f32),
            jax.ShapeDtypeStruct((1, 320), f32),
        ),
        in_specs=[pl.BlockSpec(memory_space=pl.ANY)] * 6,
        out_specs=[pl.BlockSpec(memory_space=pltpu.VMEM)] * 4,
        scratch_shapes=scratch,
        compiler_params=pltpu.CompilerParams(
            collective_id=0, has_side_effects=True, vmem_limit_bytes=56 * 1024 * 1024
        ),
    )(patches, grad_y, wt, wo, window_ids.reshape(192, 128), norm_gain.reshape(10, 128))
    return gx.T, jnp.transpose(gqkv, (1, 0, 2)), gout, ggain.reshape(320)


def solution(mesh):
    in_specs = (P("vis", None), P(), P(None, None, "head"), P(None, "head"), P("vis", None), P())
    out_specs = (P("vis", "head"), P("vis", None, "head"), P("vis", "head"), P("head"))
    return jax.shard_map(
        per_device, mesh=mesh, in_specs=in_specs, out_specs=out_specs, check_vma=False
    )
```

```python
import functools

import jax
import jax.numpy as jnp
from jax import lax
from jax.experimental import pallas as pl
from jax.experimental.pallas import tpu as pltpu
from jax.sharding import PartitionSpec as P

f32 = jnp.float32
bf16 = jnp.bfloat16
D = 1280
HD = 80
R = 384
SCALE = HD ** (-0.5)
EPS = 1e-06
MESH = pl.DeviceIdType.MESH
NEG = -1e30
WZ = 256
WX = 384
TILES = WX // 128
WAYS = {"r": 1, "l": -1}


def hops(way, half):
    return 4 if (way == "r") == (half == 0) else 3


def nn(a, b):
    return lax.dot_general(a, b, (((1,), (0,)), ((), ())), preferred_element_type=f32)


def nt(a, b, precision=None):
    return lax.dot_general(
        a, b, (((1,), (1,)), ((), ())), preferred_element_type=f32, precision=precision
    )


NAMES = ["proj", "halo0", "halo1", "nt", "gyt", "gt", "core", "gcore"]
NAMES += [f"{w}{k}{j}" for w in WAYS for k in range(2) for j in range(hops(w, k))]
NAMES += [f"xs{d}" for d in range(1, 4)]
NAMES += [f"x{t}{d}" for t in range(TILES) for d in range(1, 4)]
NAMES += [f"z{t}{d}" for t in range(TILES) for d in range(1, 8)]
NAMES += [f"{n}{d}" for n in ("y", "s", "gx", "gy") for d in range(1, 4)]
NAMES += [f"gz{d}" for d in range(1, 8)]
MSG = {name: i for i, name in enumerate(NAMES)}


def kernel(
    x_hbm, gy_hbm, wt_hbm, wo_hbm, ids_hbm, gain_hbm,
    gx_out, gqkv_out, gout_out, ggain_out,
    x_v, gy_v, wt, wo, ids, gain,
    xt, nrm, gyt, wn, gcol, inv,
    psend, proj, hsend, halo, kn, vn, idr, idc, main, sec,
    gt, at, gtr,
    pz, ring, acc, xs, xr,
    px, pxr, accx, zs, zr, csend, crecv,
    gnf, ysend, yrecv, ssend, srecv,
    gp, gxr, gcs, gcr, gzs, gzr, gys, gyr,
    lsem, send_sem, recv_sem,
):
    v = lax.axis_index("vis")
    h = lax.axis_index("head")
    c = lax.rem(v, 2)
    q = v // 2
    x = lax.rem(q, 4)
    z = v // 8
    dev = lambda zz, xx, cc: (zz * 8 + xx * 2 + cc, h)
    zdev = lambda d: dev(lax.rem(z + d + 8, 8), x, c)
    xdev = lambda d: dev(z, lax.rem(x + d, 4), c)
    ydev = lambda d: (v, lax.rem(h + d, 4))
    peer = (v + 1 - 2 * c, h)
    chip = lambda d, cc: (2 * lax.rem(q + d + 32, 32) + cc, h)

    loads = []

    def load(src, dst):
        cp = pltpu.make_async_copy(src, dst, lsem.at[len(loads)])
        cp.start()
        loads.append(cp)
        return cp

    ld_x = load(x_hbm, x_v)
    ld_gain = load(gain_hbm, gain)
    ld_gy = load(gy_hbm, gy_v)
    ld_w = []
    for k in (1, 0):
        half = c if k == 0 else 1 - c
        for comp in range(3):
            src = pl.multiple_of(320 * comp + 160 * half, 16)
            ld_w.append(load(wt_hbm.at[pl.ds(src, 160), :], wt.at[pl.ds(480 * k + 160 * comp, 160), :]))
        src = pl.multiple_of(160 * half, 16)
        ld_w.append(load(wo_hbm.at[pl.ds(src, 160), :], wo.at[pl.ds(160 * k, 160), :]))
    ld_ids = load(ids_hbm, ids)

    barrier = pltpu.get_barrier_semaphore()
    greet = [peer]
    greet += [zdev(d) for d in range(1, 8)]
    greet += [xdev(d) for d in range(1, 4)]
    greet += [ydev(d) for d in range(1, 4)]
    greet += [chip(2 * c - 1, 0), chip(2 * c - 1, 1), chip(1 - 2 * c, c)]
    for d in greet:
        pl.semaphore_signal(barrier, inc=1, device_id=d, device_id_type=MESH)

    copies = {}

    def send(name, src, dst, to):
        i = MSG[name]
        cp = pltpu.make_async_remote_copy(
            src_ref=src, dst_ref=dst, send_sem=send_sem.at[i], recv_sem=recv_sem.at[i],
            device_id=to, device_id_type=MESH,
        )
        cp.start()
        copies[name] = cp

    def arrived(name):
        copies[name].wait_recv()
    ld_x.wait()
    ld_gain.wait()
    xt[...] = x_v[...].T
    for i in range(10):
        gcol[pl.ds(128 * i, 128), :] = jnp.broadcast_to(gain[pl.ds(i, 1), :], (128, 128)).T
    for b in range(3):
        lanes = pl.ds(128 * b, 128)
        xf = xt[:, lanes].astype(f32)
        iv = lax.rsqrt(jnp.sum(xf * xf, axis=0, keepdims=True) * (1.0 / D) + EPS)
        inv[:, lanes] = iv
        nrm[:, lanes] = (xf * iv * gcol[...]).astype(bf16)
    ld_gy.wait()
    gyt[:, 0:R] = gy_v[...].T
    for cp in ld_w:
        cp.wait()
    ld_ids.wait()
    def project(half, dst):
        pa = nn(wt[pl.ds(480 * half, 480), :], nrm[:, 0:R]).astype(bf16)
        pg = nn(wo[pl.ds(160 * half, 160), :], gyt[:, 0:R]).astype(bf16)
        for b in range(3):
            dst[b, 0:480, :] = pa[:, 128 * b : 128 * b + 128]
            dst[b, 480:640, :] = pg[:, 128 * b : 128 * b + 128]

    project(1, psend)
    pl.semaphore_wait(barrier, len(greet))
    edge = 2 * c
    lane320 = lax.broadcasted_iota(jnp.int32, (320, 128), 1) < 64

    def pack_halo(k, block):
        top, low = block[0:320].astype(f32), block[320:640].astype(f32)
        first = jnp.where(lane320, top, pltpu.roll(low, 64, 1))
        last = jnp.where(lane320, pltpu.roll(top, 64, 1), low)
        hsend[k] = jnp.where(c == 0, first, last).astype(bf16)

    pack_halo(1, psend[edge])
    send("halo1", hsend.at[1], halo.at[c], chip(2 * c - 1, 1 - c))
    send("proj", psend, proj.at[pl.ds(3, 3)], peer)
    project(0, proj)
    pack_halo(0, proj[edge])
    send("halo0", hsend.at[0], halo.at[c], chip(2 * c - 1, c))
    send("gyt", gyt.at[:, pl.ds(0, R)], gyt.at[:, pl.ds(R, R)], peer)
    send("nt", nrm.at[:, pl.ds(0, R)], nrm.at[:, pl.ds(R, R)], peer)
    for s in range(3):
        idr[pl.ds(s, 1), :] = ids[pl.ds(6 * q + 3 * c + s, 1), :]
        idr[pl.ds(3 + s, 1), :] = ids[pl.ds(6 * q + 3 - 3 * c + s, 1), :]
    lane1 = lax.broadcasted_iota(jnp.int32, (1, 128), 1) < 64
    after = ids[pl.ds(lax.rem(6 * q + 6, 192), 1), :]
    before = ids[pl.ds(lax.rem(6 * q + 191, 192), 1), :]
    idr[pl.ds(6, 1), :] = jnp.where(lane1, after, before)
    for s in range(7):
        idc[s] = jnp.broadcast_to(idr[pl.ds(s, 1), :], (128, 128)).T

    wn[...] = wt[...].T

    def natural(s):
        kn[s] = proj[s, 160:320, :].T
        vn[s] = proj[s, 320:480, :].T

    for s in range(3):
        natural(s)
    arrived("proj")
    for s in range(3, 6):
        natural(s)

    pick = lambda a, b: jnp.where(c == 0, a, b) if a != b else a
    nxt = [pick(*p) for p in ((1, 1), (2, 2), (3, 6), (4, 4), (5, 5), (6, 0), (0, 3))]
    prv = [pick(*p) for p in ((6, 5), (0, 0), (1, 1), (2, 6), (3, 3), (4, 4), (5, 2))]
    lane160 = lax.broadcasted_iota(jnp.int32, (160, 128), 1) < 64
    zero = jnp.zeros((HD, 128), bf16)

    def diagonal(t):
        return jnp.concatenate(
            [jnp.concatenate([t[0:80], zero], axis=1), jnp.concatenate([zero, t[80:160]], axis=1)], axis=0
        )

    def diag_of(t):
        return jnp.concatenate([t[0:80, 0:128], t[80:160, 128:256]], axis=0)

    def attend(s, n, p, inside=True):
        q2, g2 = diagonal(proj[s, 0:160, :]), diagonal(proj[s, 480:640, :])
        kt, vt = [
            jnp.concatenate(
                [
                    proj[s, w : w + 160, :],
                    jnp.where(lane160, proj[n, w : w + 160, :].astype(f32), proj[p, w : w + 160, :].astype(f32)).astype(bf16),
                ],
                axis=1,
            )
            for w in (160, 320)
        ]
        kk, vv = [jnp.concatenate([t[s], t[n, 0:64], t[p, 64:128]], axis=0) for t in (kn, vn)]
        key_ids = jnp.concatenate([idc[s], idc[n, 0:64], idc[p, 64:128]], axis=0)
        same = key_ids == idr[pl.ds(s, 1), :]
        same = jnp.concatenate([same, same], axis=1)
        scores = jnp.where(same, nn(kk, q2) * SCALE, NEG)
        e = jnp.exp(scores - jnp.max(scores, axis=0, keepdims=True))
        w = e * (1.0 / jnp.sum(e, axis=0, keepdims=True))
        probs = w.astype(bf16)
        att = diag_of(nn(vt, probs)).astype(bf16)
        both = att.astype(f32) * proj[s, 480:640, :].astype(f32)
        delta = jnp.concatenate(
            [jnp.sum(both[0:80], axis=0, keepdims=True), jnp.sum(both[80:160], axis=0, keepdims=True)], axis=1
        )
        ds = (w * (nn(vv, g2) - delta) * SCALE).astype(bf16)
        if inside:
            lanes = pl.ds(pl.multiple_of(128 * s, 128), 128)
            at[:, lanes] = att
            gt[0:160, lanes] = diag_of(nn(kt, ds)).astype(bf16)
        gk = nt(q2, ds)
        gv = nt(g2, probs)
        main[s, 0:160, :] = gk[:, 0:128]
        main[s, 160:320, :] = gv[:, 0:128]
        sec[s, 0:160, :] = gk[:, 128:256]
        sec[s, 160:320, :] = gv[:, 128:256]

    attend(1, 2, 0)
    attend(pick(2, 0), pick(3, 1), pick(1, 5))
    attend(pick(3, 5), pick(4, 0), pick(2, 4))
    attend(4, 5, 3)

    arrived("halo0")
    arrived("halo1")
    ha, hb = halo[0].astype(f32), halo[1].astype(f32)
    proj[6, 0:320, :] = jnp.where(lane320, ha, pltpu.roll(hb, 64, 1)).astype(bf16)
    proj[6, 320:640, :] = jnp.where(lane320, pltpu.roll(ha, 64, 1), hb).astype(bf16)
    natural(6)
    attend(pick(0, 2), pick(1, 6), pick(6, 1))
    attend(pick(5, 3), pick(6, 4), pick(4, 6))
    attend(6, nxt[6], prv[6], inside=False)
    lane320 = lax.broadcasted_iota(jnp.int32, (320, 128), 1) < 64
    for s in (3, 4, 5, 0, 1, 2):
        total = main[s] + jnp.where(lane320, sec[prv[s]], sec[nxt[s]])
        gt[160:480, 128 * s : 128 * s + 128] = total.astype(bf16)
        if s == 5:
            send("gt", gt.at[:, pl.ds(R, R)], gtr, peer)

    def ring_send(way, k, j):
        n = hops(way, k)
        chunk = lax.rem(z + 8 + WAYS[way] * (n - j), 8)
        slot = ring.at[4 * (2 * (way == "l") + k) + j]
        send(f"{way}{k}{j}", pz.at[chunk, pl.ds(80 * k, 80)], slot, zdev(WAYS[way]))

    def ring_add(j):
        for k in range(2):
            for way in WAYS:
                n = hops(way, k)
                if j < n - 1:
                    arrived(f"{way}{k}{j}")
                    chunk = lax.rem(z + 8 + WAYS[way] * (n - 1 - j), 8)
                    rows = pl.ds(80 * k, 80)
                    got = ring[4 * (2 * (way == "l") + k) + j]
                    pz[chunk, rows] = (pz[chunk, rows].astype(f32) + got.astype(f32)).astype(bf16)
                    ring_send(way, k, j + 1)

    def ring_end():
        for k in range(2):
            total = pz[z, pl.ds(80 * k, 80)].astype(f32)
            for way in WAYS:
                j = hops(way, k) - 1
                arrived(f"{way}{k}{j}")
                total = total + ring[4 * (2 * (way == "l") + k) + j].astype(f32)
            for i in range(2):
                piece = total[40 * i : 40 * i + 40]
                acc[2 * k + i] = piece
                xs[2 * k + i] = jnp.concatenate([piece, jnp.zeros((8, WZ), f32)], axis=0).astype(bf16)
        for d in (2, 1, 3):
            send(f"xs{d}", xs.at[lax.rem(x + d, 4)], xr.at[d - 1], xdev(d))

    def x_sum(t):
        total = px[t, x].astype(f32)
        for d in range(1, 4):
            arrived(f"x{t}{d}")
            total = total + pxr[t, d - 1].astype(f32)
        for i in range(8):
            piece = total[40 * i : 40 * i + 40]
            accx[t, i] = piece
            zs[t, i] = jnp.concatenate([piece, jnp.zeros((8, 128), f32)], axis=0).astype(bf16)
        for d in (4, 3, 5, 2, 6, 1, 7):
            send(f"z{t}{d}", zs.at[t, lax.rem(z + d, 8)], zr.at[t, d - 1], zdev(d))

    def z_sum(t):
        total = accx[t, z]
        for d in range(1, 8):
            arrived(f"z{t}{d}")
            total = total + zr[t, d - 1].astype(f32)[0:40]
        return total

    arrived("gyt")
    arrived("nt")
    first_z = nt(nrm[...], gt[0:WZ, :]).astype(bf16)
    for i in range(8):
        pz[i] = first_z[160 * i : 160 * i + 160]
    for k in range(2):
        for way in WAYS:
            ring_send(way, k, 0)
    first_x = jnp.concatenate([nt(nrm[...], gt[WZ:480, :]), nt(gyt[...], at[...])], axis=1)
    for i in range(4):
        rows = [first_x[160 * j + 40 * i : 160 * j + 40 * i + 40] for j in range(8)]
        rows = jnp.concatenate(rows, axis=0).astype(bf16)
        for t in range(TILES):
            px[t, i] = rows[:, 128 * t : 128 * t + 128]
    for t in range(TILES):
        for d in (2, 1, 3):
            send(f"x{t}{d}", px.at[t, lax.rem(x + d, 4)], pxr.at[t, d - 1], xdev(d))

    arrived("gt")
    ssum = jnp.zeros((1, R), f32)
    gp[...] = jnp.zeros((8, 320), f32)
    ones = jnp.ones((8, 128), bf16)
    for d in (2, 1, 3, 0):
        to = lax.rem(h + d, 4)
        rows = pl.ds(pl.multiple_of(320 * to, 64), 320)
        g = nn(wn[rows, 0:480], gt[:, 0:R]) + nn(wn[rows, 480:960], gtr[...])
        if d:
            ysend[d - 1] = g.astype(bf16)
            send(f"y{d}", ysend.at[d - 1], yrecv.at[d - 1], ydev(d))
        else:
            gnf[...] = g
        parts = []
        gains = jnp.zeros((320, 128), f32)
        for b in range(3):
            lanes = slice(128 * b, 128 * b + 128)
            gb = g[:, lanes] * xt[rows, lanes].astype(f32)
            parts.append(jnp.sum(gb * gcol[rows, :], axis=0, keepdims=True))
            gains = gains + gb * inv[:, lanes]
        ssum = ssum + jnp.concatenate(parts, axis=1)
        high = gains.astype(bf16)
        low = (gains - high.astype(f32)).astype(bf16)
        gp[pl.ds(to, 1), :] = (nt(ones, high) + nt(ones, low))[0:1]
    ssend[...] = jnp.broadcast_to(ssum, (8, R))
    for d in range(1, 4):
        send(f"s{d}", ssend, srecv.at[d - 1], ydev(d))
    for d in range(1, 4):
        send(f"gx{d}", gp, gxr.at[d - 1], xdev(d))
    ring_add(0)
    x_sum(0)
    ring_add(1)
    total = gp[...]
    for d in range(1, 4):
        arrived(f"gx{d}")
        total = total + gxr[d - 1]
    gcs[...] = total
    send("gcore", gcs, gcr, peer)
    x_sum(1)
    ring_add(2)
    arrived("gcore")
    gzs[...] = gcs[...] + gcr[...]
    for d in range(1, 8):
        send(f"gz{d}", gzs, gzr.at[d - 1], zdev(d))
    x_sum(2)
    ring_end()

    mine = pl.ds(pl.multiple_of(320 * h, 64), 320)
    gn = gnf[...]
    sums = ssum
    for d in range(1, 4):
        arrived(f"y{d}")
        arrived(f"s{d}")
        gn = gn + yrecv[d - 1].astype(f32)
        sums = sums + srecv[d - 1, 0:1, :]
    iv = inv[...]
    gc = jnp.concatenate([gcol[mine, :]] * 3, axis=1)
    xi = xt[mine, :].astype(f32) * iv
    gx = gyt[mine, 0:R].astype(f32) + iv * (gn * gc - xi * (iv * (sums * (1.0 / D))))
    gx_out[...] = gx.astype(bf16)

    total = gzs[...]
    for d in range(1, 8):
        arrived(f"gz{d}")
        total = total + gzr[d - 1]
    gys[...] = total
    for d in range(1, 4):
        send(f"gy{d}", gys, gyr.at[d - 1], ydev(d))

    parts = [None] + [z_sum(t) for t in range(TILES)]
    total = acc[x]
    for d in range(1, 4):
        arrived(f"xs{d}")
        total = total + xr[d - 1].astype(f32)[0:40]
    parts[0] = total
    both = jnp.concatenate(parts, axis=1)
    low, high = both[0:20], both[20:40]
    first = c == 0
    csend[0:20, :] = jnp.where(first, high, low)
    csend[20:24, :] = jnp.zeros((4, 640), f32)
    send("core", csend, crecv, peer)
    own = jnp.where(first, low, high)
    total = gys[pl.ds(h, 1), :]
    for d in range(1, 4):
        arrived(f"gy{d}")
        total = total + gyr[d - 1, pl.ds(h, 1), :]
    ggain_out[...] = total[0]
    arrived("core")
    other = crecv[0:20, :]
    sides = (jnp.where(first, own, other), jnp.where(first, other, own))
    for i, side in enumerate(sides):
        cols = slice(160 * i, 160 * i + 160)
        for comp in range(3):
            gqkv_out[comp, :, cols] = side[:, 160 * comp : 160 * comp + 160]
        gout_out[:, cols] = side[:, 480:640]
    for cp in copies.values():
        cp.wait_send()


def hand_over(*refs):
    for src, dst in zip(refs[:4], refs[4:]):
        dst[...] = src[...]


def per_device(patches, norm_gain, w_qkv, w_out, grad_y, window_ids):
    wt = jnp.transpose(w_qkv, (1, 2, 0)).reshape(960, D)
    wo = jnp.transpose(w_out)
    V = pltpu.VMEM
    scratch = [
        V((R, D), bf16), V((R, D), bf16), V((960, D), bf16), V((320, D), bf16),
        V((192, 128), jnp.int32), V((10, 128), f32),
        V((D, R), bf16), V((D, 2 * R), bf16), V((D, 2 * R), bf16), V((D, 960), bf16),
        V((D, 128), f32), V((1, R), f32),
        V((3, 640, 128), bf16), V((7, 640, 128), bf16), V((2, 320, 128), bf16), V((2, 320, 128), bf16),
        V((7, 128, 160), bf16), V((7, 128, 160), bf16),
        V((8, 128), jnp.int32), V((7, 128, 128), jnp.int32),
        V((7, 320, 128), f32), V((7, 320, 128), f32),
        V((480, 2 * R), bf16), V((160, 2 * R), bf16), V((480, R), bf16),
        V((8, 160, WZ), bf16), V((16, 80, WZ), bf16),
        V((4, 40, WZ), f32), V((4, 48, WZ), bf16), V((3, 48, WZ), bf16),
        V((TILES, 4, 320, 128), bf16), V((TILES, 3, 320, 128), bf16),
        V((TILES, 8, 40, 128), f32), V((TILES, 8, 48, 128), bf16), V((TILES, 7, 48, 128), bf16),
        V((24, 640), f32), V((24, 640), f32),
        V((320, R), f32), V((3, 320, R), bf16), V((3, 320, R), bf16),
        V((8, R), f32), V((3, 8, R), f32),
        V((8, 320), f32), V((3, 8, 320), f32), V((8, 320), f32), V((8, 320), f32),
        V((8, 320), f32), V((7, 8, 320), f32), V((8, 320), f32), V((3, 8, 320), f32),
        pltpu.SemaphoreType.DMA((12,)),
        pltpu.SemaphoreType.DMA((len(NAMES),)),
        pltpu.SemaphoreType.DMA((len(NAMES),)),
    ]
    results = pl.pallas_call(
        kernel,
        out_shape=(
            jax.ShapeDtypeStruct((320, R), bf16),
            jax.ShapeDtypeStruct((3, 20, 320), f32),
            jax.ShapeDtypeStruct((20, 320), f32),
            jax.ShapeDtypeStruct((320,), f32),
        ),
        in_specs=[pl.BlockSpec(memory_space=pl.ANY)] * 6,
        out_specs=[pl.BlockSpec(memory_space=pltpu.VMEM)] * 4,
        scratch_shapes=scratch,
        compiler_params=pltpu.CompilerParams(
            collective_id=0, has_side_effects=True, vmem_limit_bytes=56 * 1024 * 1024
        ),
    )(patches, grad_y, wt, wo, window_ids.reshape(192, 128), norm_gain.reshape(10, 128))
    vmem = pl.BlockSpec(memory_space=pltpu.VMEM)
    gx, gqkv, gout, ggain = pl.pallas_call(
        hand_over,
        out_shape=tuple(jax.ShapeDtypeStruct(r.shape, r.dtype) for r in results),
        in_specs=[vmem] * 4,
        out_specs=[vmem] * 4,
    )(*results)
    return gx.T, jnp.transpose(gqkv, (1, 0, 2)), gout, ggain


def solution(mesh):
    in_specs = (P("vis", None), P(), P(None, None, "head"), P(None, "head"), P("vis", None), P())
    out_specs = (P("vis", "head"), P("vis", None, "head"), P("vis", "head"), P("head"))
    return jax.shard_map(
        per_device, mesh=mesh, in_specs=in_specs, out_specs=out_specs, check_vma=False
    )
```

```python
import functools

import jax
import jax.numpy as jnp
from jax import lax
from jax.experimental import pallas as pl
from jax.experimental.pallas import tpu as pltpu
from jax.sharding import PartitionSpec as P

f32 = jnp.float32
bf16 = jnp.bfloat16
D = 1280
HD = 80
R = 384
SCALE = HD ** (-0.5)
EPS = 1e-06
MESH = pl.DeviceIdType.MESH
NEG = -1e30
WZ = 256
WX = 384
TILES = WX // 128
WAYS = (1, -1)


def nn(a, b):
    return lax.dot_general(a, b, (((1,), (0,)), ((), ())), preferred_element_type=f32)


def nt(a, b, precision=None):
    return lax.dot_general(
        a, b, (((1,), (1,)), ((), ())), preferred_element_type=f32, precision=precision
    )


NAMES = ["proj", "halo0", "halo1", "nt", "gyt", "gt", "core", "gcore"]
NAMES += [f"z{n}{w}" for n in "ahnb" for w in range(2)]
NAMES += [f"xs{d}" for d in range(1, 4)]
NAMES += [f"x{n}{t}{w}" for n in "ab" for t in range(TILES) for w in range(2)]
NAMES += [f"z{t}{d}" for t in range(TILES) for d in range(1, 8)]
NAMES += [f"{n}{d}" for n in ("y", "s", "gx", "gy") for d in range(1, 4)]
NAMES += [f"gz{d}" for d in range(1, 8)]
MSG = {name: i for i, name in enumerate(NAMES)}


def kernel(
    x_hbm, gy_hbm, wt_hbm, wo_hbm, ids_hbm, gain_hbm,
    gx_out, gqkv_out, gout_out, ggain_out,
    x_v, gy_v, wt, wo, ids, gain,
    xt, nrm, gyt, wn, gcol, inv,
    psend, proj, hsend, halo, kn, vn, idr, idc, main, sec,
    gt, at, gtr,
    pz, za, zh, zn, zb, acc, xs, xr,
    px, xa, xb, accx, zs, zr, csend, crecv,
    gnf, ysend, yrecv, ssend, srecv,
    gp, gxr, gcs, gcr, gzs, gzr, gys, gyr,
    lsem, send_sem, recv_sem,
):
    v = lax.axis_index("vis")
    h = lax.axis_index("head")
    c = lax.rem(v, 2)
    q = v // 2
    x = lax.rem(q, 4)
    z = v // 8
    dev = lambda zz, xx, cc: (zz * 8 + xx * 2 + cc, h)
    zdev = lambda d: dev(lax.rem(z + d + 8, 8), x, c)
    xdev = lambda d: dev(z, lax.rem(x + d + 4, 4), c)
    ydev = lambda d: (v, lax.rem(h + d, 4))
    peer = (v + 1 - 2 * c, h)
    chip = lambda d, cc: (2 * lax.rem(q + d + 32, 32) + cc, h)

    loads = []

    def load(src, dst):
        cp = pltpu.make_async_copy(src, dst, lsem.at[len(loads)])
        cp.start()
        loads.append(cp)
        return cp

    ld_x = load(x_hbm, x_v)
    ld_gain = load(gain_hbm, gain)
    ld_gy = load(gy_hbm, gy_v)
    ld_w = []
    for k in (1, 0):
        half = c if k == 0 else 1 - c
        for comp in range(3):
            src = pl.multiple_of(320 * comp + 160 * half, 16)
            ld_w.append(load(wt_hbm.at[pl.ds(src, 160), :], wt.at[pl.ds(480 * k + 160 * comp, 160), :]))
        src = pl.multiple_of(160 * half, 16)
        ld_w.append(load(wo_hbm.at[pl.ds(src, 160), :], wo.at[pl.ds(160 * k, 160), :]))
    ld_ids = load(ids_hbm, ids)

    barrier = pltpu.get_barrier_semaphore()
    greet = [peer]
    greet += [zdev(d) for d in range(1, 8)]
    greet += [xdev(d) for d in range(1, 4)]
    greet += [ydev(d) for d in range(1, 4)]
    greet += [chip(2 * c - 1, 0), chip(2 * c - 1, 1), chip(1 - 2 * c, c)]
    for d in greet:
        pl.semaphore_signal(barrier, inc=1, device_id=d, device_id_type=MESH)

    copies = {}

    def send(name, src, dst, to):
        i = MSG[name]
        cp = pltpu.make_async_remote_copy(
            src_ref=src, dst_ref=dst, send_sem=send_sem.at[i], recv_sem=recv_sem.at[i],
            device_id=to, device_id_type=MESH,
        )
        cp.start()
        copies[name] = cp

    def arrived(name):
        copies[name].wait_recv()
    ld_x.wait()
    ld_gain.wait()
    xt[...] = x_v[...].T
    for i in range(10):
        gcol[pl.ds(128 * i, 128), :] = jnp.broadcast_to(gain[pl.ds(i, 1), :], (128, 128)).T
    for b in range(3):
        lanes = pl.ds(128 * b, 128)
        xf = xt[:, lanes].astype(f32)
        iv = lax.rsqrt(jnp.sum(xf * xf, axis=0, keepdims=True) * (1.0 / D) + EPS)
        inv[:, lanes] = iv
        nrm[:, lanes] = (xf * iv * gcol[...]).astype(bf16)
    ld_gy.wait()
    gyt[:, 0:R] = gy_v[...].T
    for cp in ld_w:
        cp.wait()
    ld_ids.wait()
    def project(half, dst):
        pa = nn(wt[pl.ds(480 * half, 480), :], nrm[:, 0:R]).astype(bf16)
        pg = nn(wo[pl.ds(160 * half, 160), :], gyt[:, 0:R]).astype(bf16)
        for b in range(3):
            dst[b, 0:480, :] = pa[:, 128 * b : 128 * b + 128]
            dst[b, 480:640, :] = pg[:, 128 * b : 128 * b + 128]

    project(1, psend)
    pl.semaphore_wait(barrier, len(greet))
    edge = 2 * c
    lane320 = lax.broadcasted_iota(jnp.int32, (320, 128), 1) < 64

    def pack_halo(k, block):
        top, low = block[0:320].astype(f32), block[320:640].astype(f32)
        first = jnp.where(lane320, top, pltpu.roll(low, 64, 1))
        last = jnp.where(lane320, pltpu.roll(top, 64, 1), low)
        hsend[k] = jnp.where(c == 0, first, last).astype(bf16)

    pack_halo(1, psend[edge])
    send("halo1", hsend.at[1], halo.at[c], chip(2 * c - 1, 1 - c))
    send("proj", psend, proj.at[pl.ds(3, 3)], peer)
    project(0, proj)
    pack_halo(0, proj[edge])
    send("halo0", hsend.at[0], halo.at[c], chip(2 * c - 1, c))
    send("gyt", gyt.at[:, pl.ds(0, R)], gyt.at[:, pl.ds(R, R)], peer)
    send("nt", nrm.at[:, pl.ds(0, R)], nrm.at[:, pl.ds(R, R)], peer)
    for s in range(3):
        idr[pl.ds(s, 1), :] = ids[pl.ds(6 * q + 3 * c + s, 1), :]
        idr[pl.ds(3 + s, 1), :] = ids[pl.ds(6 * q + 3 - 3 * c + s, 1), :]
    lane1 = lax.broadcasted_iota(jnp.int32, (1, 128), 1) < 64
    after = ids[pl.ds(lax.rem(6 * q + 6, 192), 1), :]
    before = ids[pl.ds(lax.rem(6 * q + 191, 192), 1), :]
    idr[pl.ds(6, 1), :] = jnp.where(lane1, after, before)
    for s in range(7):
        idc[s] = jnp.broadcast_to(idr[pl.ds(s, 1), :], (128, 128)).T

    wn[...] = wt[...].T

    def natural(s):
        kn[s] = proj[s, 160:320, :].T
        vn[s] = proj[s, 320:480, :].T

    for s in range(3):
        natural(s)
    arrived("proj")
    for s in range(3, 6):
        natural(s)

    pick = lambda a, b: jnp.where(c == 0, a, b) if a != b else a
    nxt = [pick(*p) for p in ((1, 1), (2, 2), (3, 6), (4, 4), (5, 5), (6, 0), (0, 3))]
    prv = [pick(*p) for p in ((6, 5), (0, 0), (1, 1), (2, 6), (3, 3), (4, 4), (5, 2))]
    lane160 = lax.broadcasted_iota(jnp.int32, (160, 128), 1) < 64
    zero = jnp.zeros((HD, 128), bf16)

    def diagonal(t):
        return jnp.concatenate(
            [jnp.concatenate([t[0:80], zero], axis=1), jnp.concatenate([zero, t[80:160]], axis=1)], axis=0
        )

    def diag_of(t):
        return jnp.concatenate([t[0:80, 0:128], t[80:160, 128:256]], axis=0)

    def attend(s, n, p, inside=True):
        q2, g2 = diagonal(proj[s, 0:160, :]), diagonal(proj[s, 480:640, :])
        kt, vt = [
            jnp.concatenate(
                [
                    proj[s, w : w + 160, :],
                    jnp.where(lane160, proj[n, w : w + 160, :].astype(f32), proj[p, w : w + 160, :].astype(f32)).astype(bf16),
                ],
                axis=1,
            )
            for w in (160, 320)
        ]
        kk, vv = [jnp.concatenate([t[s], t[n, 0:64], t[p, 64:128]], axis=0) for t in (kn, vn)]
        key_ids = jnp.concatenate([idc[s], idc[n, 0:64], idc[p, 64:128]], axis=0)
        same = key_ids == idr[pl.ds(s, 1), :]
        same = jnp.concatenate([same, same], axis=1)
        scores = jnp.where(same, nn(kk, q2) * SCALE, NEG)
        e = jnp.exp(scores - jnp.max(scores, axis=0, keepdims=True))
        w = e * (1.0 / jnp.sum(e, axis=0, keepdims=True))
        probs = w.astype(bf16)
        att = diag_of(nn(vt, probs)).astype(bf16)
        both = att.astype(f32) * proj[s, 480:640, :].astype(f32)
        delta = jnp.concatenate(
            [jnp.sum(both[0:80], axis=0, keepdims=True), jnp.sum(both[80:160], axis=0, keepdims=True)], axis=1
        )
        ds = (w * (nn(vv, g2) - delta) * SCALE).astype(bf16)
        if inside:
            lanes = pl.ds(pl.multiple_of(128 * s, 128), 128)
            at[:, lanes] = att
            gt[0:160, lanes] = diag_of(nn(kt, ds)).astype(bf16)
        gk = nt(q2, ds)
        gv = nt(g2, probs)
        main[s, 0:160, :] = gk[:, 0:128]
        main[s, 160:320, :] = gv[:, 0:128]
        sec[s, 0:160, :] = gk[:, 128:256]
        sec[s, 160:320, :] = gv[:, 128:256]

    attend(1, 2, 0)
    attend(pick(2, 0), pick(3, 1), pick(1, 5))
    attend(pick(3, 5), pick(4, 0), pick(2, 4))
    attend(4, 5, 3)

    arrived("halo0")
    arrived("halo1")
    ha, hb = halo[0].astype(f32), halo[1].astype(f32)
    proj[6, 0:320, :] = jnp.where(lane320, ha, pltpu.roll(hb, 64, 1)).astype(bf16)
    proj[6, 320:640, :] = jnp.where(lane320, pltpu.roll(ha, 64, 1), hb).astype(bf16)
    natural(6)
    attend(pick(0, 2), pick(1, 6), pick(6, 1))
    attend(pick(5, 3), pick(6, 4), pick(4, 6))
    attend(6, nxt[6], prv[6], inside=False)
    lane320 = lax.broadcasted_iota(jnp.int32, (320, 128), 1) < 64
    for s in (3, 4, 5, 0, 1, 2):
        total = main[s] + jnp.where(lane320, sec[prv[s]], sec[nxt[s]])
        gt[160:480, 128 * s : 128 * s + 128] = total.astype(bf16)
        if s == 5:
            send("gt", gt.at[:, pl.ds(R, R)], gtr, peer)

    def z_start():
        for w, way in enumerate(WAYS):
            send(f"za{w}", pz.at[lax.rem(z + 8 + 3 * way, 8)], za.at[w], zdev(way))
        for w, way in enumerate(WAYS):
            send(f"zh{w}", pz.at[lax.rem(z + 4, 8), pl.ds(80 * w, 80)], zh.at[w], zdev(2 * way))
        for w, way in enumerate(WAYS):
            send(f"zn{w}", pz.at[lax.rem(z + 8 + way, 8)], zn.at[w], zdev(way))

    def z_pass():
        for w, way in enumerate(WAYS):
            arrived(f"za{w}")
            arrived(f"zh{w}")
            chunk = lax.rem(z + 8 + 2 * way, 8)
            for k in range(2):
                rows = pl.ds(80 * k, 80)
                total = pz[chunk, rows].astype(f32) + za[w, rows].astype(f32)
                if k == w:
                    total = total + zh[w].astype(f32)
                pz[chunk, rows] = total.astype(bf16)
            send(f"zb{w}", pz.at[chunk], zb.at[w], zdev(2 * way))

    def z_end():
        total = pz[z].astype(f32)
        for w in range(2):
            arrived(f"zn{w}")
            arrived(f"zb{w}")
            total = total + zn[w].astype(f32) + zb[w].astype(f32)
        for i in range(4):
            piece = total[40 * i : 40 * i + 40]
            acc[i] = piece
            xs[i] = jnp.concatenate([piece, jnp.zeros((8, WZ), f32)], axis=0).astype(bf16)
        for d in (2, 1, 3):
            send(f"xs{d}", xs.at[lax.rem(x + d, 4)], xr.at[d - 1], xdev(d))

    def x_start(t):
        for w, way in enumerate(WAYS):
            send(f"xa{t}{w}", px.at[t, lax.rem(x + 2, 4), pl.ds(160 * w, 160)], xa.at[t, w], xdev(way))

    def x_pass(t):
        for w, way in enumerate(WAYS):
            arrived(f"xa{t}{w}")
            chunk, rows = lax.rem(x + 4 + way, 4), pl.ds(160 * w, 160)
            px[t, chunk, rows] = (px[t, chunk, rows].astype(f32) + xa[t, w].astype(f32)).astype(bf16)
            send(f"xb{t}{w}", px.at[t, chunk], xb.at[t, w], xdev(way))

    def x_sum(t):
        arrived(f"xb{t}0")
        arrived(f"xb{t}1")
        total = px[t, x].astype(f32) + xb[t, 0].astype(f32) + xb[t, 1].astype(f32)
        for i in range(8):
            piece = total[40 * i : 40 * i + 40]
            accx[t, i] = piece
            zs[t, i] = jnp.concatenate([piece, jnp.zeros((8, 128), f32)], axis=0).astype(bf16)
        for d in (4, 3, 5, 2, 6, 1, 7):
            send(f"z{t}{d}", zs.at[t, lax.rem(z + d, 8)], zr.at[t, d - 1], zdev(d))

    def z_sum(t):
        total = accx[t, z]
        for d in range(1, 8):
            arrived(f"z{t}{d}")
            total = total + zr[t, d - 1].astype(f32)[0:40]
        return total

    arrived("gyt")
    arrived("nt")
    first_z = nt(nrm[...], gt[0:WZ, :]).astype(bf16)
    for i in range(8):
        pz[i] = first_z[160 * i : 160 * i + 160]
    z_start()
    first_x = jnp.concatenate([nt(nrm[...], gt[WZ:480, :]), nt(gyt[...], at[...])], axis=1)
    for i in range(4):
        rows = [first_x[160 * j + 40 * i : 160 * j + 40 * i + 40] for j in range(8)]
        rows = jnp.concatenate(rows, axis=0).astype(bf16)
        for t in range(TILES):
            px[t, i] = rows[:, 128 * t : 128 * t + 128]
    for t in range(TILES):
        x_start(t)

    arrived("gt")
    ssum = jnp.zeros((1, R), f32)
    gp[...] = jnp.zeros((8, 320), f32)
    ones = jnp.ones((8, 128), bf16)
    for d in (2, 1, 3, 0):
        to = lax.rem(h + d, 4)
        rows = pl.ds(pl.multiple_of(320 * to, 64), 320)
        g = nn(wn[rows, 0:480], gt[:, 0:R]) + nn(wn[rows, 480:960], gtr[...])
        if d:
            ysend[d - 1] = g.astype(bf16)
            send(f"y{d}", ysend.at[d - 1], yrecv.at[d - 1], ydev(d))
        else:
            gnf[...] = g
        parts = []
        gains = jnp.zeros((320, 128), f32)
        for b in range(3):
            lanes = slice(128 * b, 128 * b + 128)
            gb = g[:, lanes] * xt[rows, lanes].astype(f32)
            parts.append(jnp.sum(gb * gcol[rows, :], axis=0, keepdims=True))
            gains = gains + gb * inv[:, lanes]
        ssum = ssum + jnp.concatenate(parts, axis=1)
        high = gains.astype(bf16)
        low = (gains - high.astype(f32)).astype(bf16)
        gp[pl.ds(to, 1), :] = (nt(ones, high) + nt(ones, low))[0:1]
    ssend[...] = jnp.broadcast_to(ssum, (8, R))
    for d in range(1, 4):
        send(f"s{d}", ssend, srecv.at[d - 1], ydev(d))
    for d in range(1, 4):
        send(f"gx{d}", gp, gxr.at[d - 1], xdev(d))
    for t in range(TILES):
        x_pass(t)
    total = gp[...]
    for d in range(1, 4):
        arrived(f"gx{d}")
        total = total + gxr[d - 1]
    gcs[...] = total
    send("gcore", gcs, gcr, peer)
    z_pass()
    arrived("gcore")
    gzs[...] = gcs[...] + gcr[...]
    for d in (4, 3, 5, 2, 6, 1, 7):
        send(f"gz{d}", gzs, gzr.at[d - 1], zdev(d))
    for t in range(TILES):
        x_sum(t)
    total = gzs[...]
    for d in range(1, 8):
        arrived(f"gz{d}")
        total = total + gzr[d - 1]
    gys[...] = total
    for d in range(1, 4):
        send(f"gy{d}", gys, gyr.at[d - 1], ydev(d))
    z_end()

    mine = pl.ds(pl.multiple_of(320 * h, 64), 320)
    gn = gnf[...]
    sums = ssum
    for d in range(1, 4):
        arrived(f"y{d}")
        arrived(f"s{d}")
        gn = gn + yrecv[d - 1].astype(f32)
        sums = sums + srecv[d - 1, 0:1, :]
    iv = inv[...]
    gc = jnp.concatenate([gcol[mine, :]] * 3, axis=1)
    xi = xt[mine, :].astype(f32) * iv
    gx = gyt[mine, 0:R].astype(f32) + iv * (gn * gc - xi * (iv * (sums * (1.0 / D))))
    gx_out[...] = gx.astype(bf16)

    parts = [None] + [z_sum(t) for t in range(TILES)]
    total = acc[x]
    for d in range(1, 4):
        arrived(f"xs{d}")
        total = total + xr[d - 1].astype(f32)[0:40]
    parts[0] = total
    both = jnp.concatenate(parts, axis=1)
    low, high = both[0:20], both[20:40]
    first = c == 0
    csend[0:20, :] = jnp.where(first, high, low)
    csend[20:24, :] = jnp.zeros((4, 640), f32)
    send("core", csend, crecv, peer)
    own = jnp.where(first, low, high)
    total = gys[pl.ds(h, 1), :]
    for d in range(1, 4):
        arrived(f"gy{d}")
        total = total + gyr[d - 1, pl.ds(h, 1), :]
    ggain_out[...] = total[0]
    arrived("core")
    other = crecv[0:20, :]
    sides = (jnp.where(first, own, other), jnp.where(first, other, own))
    for i, side in enumerate(sides):
        cols = slice(160 * i, 160 * i + 160)
        for comp in range(3):
            gqkv_out[comp, :, cols] = side[:, 160 * comp : 160 * comp + 160]
        gout_out[:, cols] = side[:, 480:640]
    for cp in copies.values():
        cp.wait_send()


def hand_over(*refs):
    for src, dst in zip(refs[:4], refs[4:]):
        dst[...] = src[...]


def per_device(patches, norm_gain, w_qkv, w_out, grad_y, window_ids):
    wt = jnp.transpose(w_qkv, (1, 2, 0)).reshape(960, D)
    wo = jnp.transpose(w_out)
    V = pltpu.VMEM
    scratch = [
        V((R, D), bf16), V((R, D), bf16), V((960, D), bf16), V((320, D), bf16),
        V((192, 128), jnp.int32), V((10, 128), f32),
        V((D, R), bf16), V((D, 2 * R), bf16), V((D, 2 * R), bf16), V((D, 960), bf16),
        V((D, 128), f32), V((1, R), f32),
        V((3, 640, 128), bf16), V((7, 640, 128), bf16), V((2, 320, 128), bf16), V((2, 320, 128), bf16),
        V((7, 128, 160), bf16), V((7, 128, 160), bf16),
        V((8, 128), jnp.int32), V((7, 128, 128), jnp.int32),
        V((7, 320, 128), f32), V((7, 320, 128), f32),
        V((480, 2 * R), bf16), V((160, 2 * R), bf16), V((480, R), bf16),
        V((8, 160, WZ), bf16), V((2, 160, WZ), bf16), V((2, 80, WZ), bf16),
        V((2, 160, WZ), bf16), V((2, 160, WZ), bf16),
        V((4, 40, WZ), f32), V((4, 48, WZ), bf16), V((3, 48, WZ), bf16),
        V((TILES, 4, 320, 128), bf16), V((TILES, 2, 160, 128), bf16),
        V((TILES, 2, 320, 128), bf16),
        V((TILES, 8, 40, 128), f32), V((TILES, 8, 48, 128), bf16), V((TILES, 7, 48, 128), bf16),
        V((24, 640), f32), V((24, 640), f32),
        V((320, R), f32), V((3, 320, R), bf16), V((3, 320, R), bf16),
        V((8, R), f32), V((3, 8, R), f32),
        V((8, 320), f32), V((3, 8, 320), f32), V((8, 320), f32), V((8, 320), f32),
        V((8, 320), f32), V((7, 8, 320), f32), V((8, 320), f32), V((3, 8, 320), f32),
        pltpu.SemaphoreType.DMA((12,)),
        pltpu.SemaphoreType.DMA((len(NAMES),)),
        pltpu.SemaphoreType.DMA((len(NAMES),)),
    ]
    results = pl.pallas_call(
        kernel,
        out_shape=(
            jax.ShapeDtypeStruct((320, R), bf16),
            jax.ShapeDtypeStruct((3, 20, 320), f32),
            jax.ShapeDtypeStruct((20, 320), f32),
            jax.ShapeDtypeStruct((320,), f32),
        ),
        in_specs=[pl.BlockSpec(memory_space=pl.ANY)] * 6,
        out_specs=[pl.BlockSpec(memory_space=pltpu.VMEM)] * 4,
        scratch_shapes=scratch,
        compiler_params=pltpu.CompilerParams(
            collective_id=0, has_side_effects=True, vmem_limit_bytes=56 * 1024 * 1024
        ),
    )(patches, grad_y, wt, wo, window_ids.reshape(192, 128), norm_gain.reshape(10, 128))
    vmem = pl.BlockSpec(memory_space=pltpu.VMEM)
    gx, gqkv, gout, ggain = pl.pallas_call(
        hand_over,
        out_shape=tuple(jax.ShapeDtypeStruct(r.shape, r.dtype) for r in results),
        in_specs=[vmem] * 4,
        out_specs=[vmem] * 4,
    )(*results)
    return gx.T, jnp.transpose(gqkv, (1, 0, 2)), gout, ggain


def solution(mesh):
    in_specs = (P("vis", None), P(), P(None, None, "head"), P(None, "head"), P("vis", None), P())
    out_specs = (P("vis", "head"), P("vis", None, "head"), P("vis", "head"), P("head"))
    return jax.shard_map(
        per_device, mesh=mesh, in_specs=in_specs, out_specs=out_specs, check_vma=False
    )
```

```python
import functools

import jax
import jax.numpy as jnp
from jax import lax
from jax.experimental import pallas as pl
from jax.experimental.pallas import tpu as pltpu
from jax.sharding import PartitionSpec as P

f32 = jnp.float32
bf16 = jnp.bfloat16
D = 1280
HD = 80
R = 384
SCALE = HD ** (-0.5)
EPS = 1e-06
MESH = pl.DeviceIdType.MESH
NEG = -1e30
WZ = 128
WX = 512
TILES = WX // 128
WAYS = (1, -1)


def nn(a, b):
    return lax.dot_general(a, b, (((1,), (0,)), ((), ())), preferred_element_type=f32)


def nt(a, b, precision=None):
    return lax.dot_general(
        a, b, (((1,), (1,)), ((), ())), preferred_element_type=f32, precision=precision
    )


NAMES = ["proj", "halo0", "halo1", "nt", "gyt", "gt", "core", "gcore"]
NAMES += [f"z{n}{w}" for n in "ahnb" for w in range(2)]
NAMES += [f"xs{d}" for d in range(1, 4)]
NAMES += [f"x{n}{t}{w}" for n in "ab" for t in range(TILES) for w in range(2)]
NAMES += [f"z{t}{d}" for t in range(TILES) for d in range(1, 8)]
NAMES += [f"{n}{d}" for n in ("y", "s", "gx", "gy") for d in range(1, 4)]
NAMES += [f"gz{d}" for d in range(1, 8)]
MSG = {name: i for i, name in enumerate(NAMES)}


def kernel(
    x_hbm, gy_hbm, wt_hbm, wo_hbm, ids_hbm, gain_hbm,
    gx_out, gqkv_out, gout_out, ggain_out,
    x_v, gy_v, wt, wo, ids, gain,
    xt, nrm, gyt, wn, gcol, inv,
    psend, proj, hsend, halo, kn, vn, idr, idc, main, sec, wts, delta,
    gt, at, gtr,
    pz, za, zh, zn, zb, acc, xs, xr,
    px, xa, xb, accx, zs, zr, csend, crecv,
    gnf, ysend, yrecv, ssend, srecv,
    gp, gxr, gcs, gcr, gzs, gzr, gys, gyr,
    lsem, send_sem, recv_sem,
):
    v = lax.axis_index("vis")
    h = lax.axis_index("head")
    c = lax.rem(v, 2)
    q = v // 2
    x = lax.rem(q, 4)
    z = v // 8
    dev = lambda zz, xx, cc: (zz * 8 + xx * 2 + cc, h)
    zdev = lambda d: dev(lax.rem(z + d + 8, 8), x, c)
    xdev = lambda d: dev(z, lax.rem(x + d + 4, 4), c)
    ydev = lambda d: (v, lax.rem(h + d, 4))
    peer = (v + 1 - 2 * c, h)
    chip = lambda d, cc: (2 * lax.rem(q + d + 32, 32) + cc, h)

    loads = []

    def load(src, dst):
        cp = pltpu.make_async_copy(src, dst, lsem.at[len(loads)])
        cp.start()
        loads.append(cp)
        return cp

    ld_x = load(x_hbm, x_v)
    ld_gain = load(gain_hbm, gain)
    ld_gy = load(gy_hbm, gy_v)
    ld_w = []
    for k in (1, 0):
        half = c if k == 0 else 1 - c
        for comp in range(3):
            src = pl.multiple_of(320 * comp + 160 * half, 16)
            ld_w.append(load(wt_hbm.at[pl.ds(src, 160), :], wt.at[pl.ds(480 * k + 160 * comp, 160), :]))
        src = pl.multiple_of(160 * half, 16)
        ld_w.append(load(wo_hbm.at[pl.ds(src, 160), :], wo.at[pl.ds(160 * k, 160), :]))
    ld_ids = load(ids_hbm, ids)

    barrier = pltpu.get_barrier_semaphore()
    greet = [peer]
    greet += [zdev(d) for d in range(1, 8)]
    greet += [xdev(d) for d in range(1, 4)]
    greet += [ydev(d) for d in range(1, 4)]
    greet += [chip(2 * c - 1, 0), chip(2 * c - 1, 1), chip(1 - 2 * c, c)]
    for d in greet:
        pl.semaphore_signal(barrier, inc=1, device_id=d, device_id_type=MESH)

    copies = {}

    def send(name, src, dst, to):
        i = MSG[name]
        cp = pltpu.make_async_remote_copy(
            src_ref=src, dst_ref=dst, send_sem=send_sem.at[i], recv_sem=recv_sem.at[i],
            device_id=to, device_id_type=MESH,
        )
        cp.start()
        copies[name] = cp

    def arrived(name):
        copies[name].wait_recv()
    ld_x.wait()
    ld_gain.wait()
    xt[...] = x_v[...].T
    for i in range(10):
        gcol[pl.ds(128 * i, 128), :] = jnp.broadcast_to(gain[pl.ds(i, 1), :], (128, 128)).T
    for b in range(3):
        lanes = pl.ds(128 * b, 128)
        xf = xt[:, lanes].astype(f32)
        iv = lax.rsqrt(jnp.sum(xf * xf, axis=0, keepdims=True) * (1.0 / D) + EPS)
        inv[:, lanes] = iv
        nrm[:, lanes] = (xf * iv * gcol[...]).astype(bf16)
    ld_gy.wait()
    gyt[:, 0:R] = gy_v[...].T
    for cp in ld_w:
        cp.wait()
    ld_ids.wait()
    def project(half, dst):
        pa = nn(wt[pl.ds(480 * half, 480), :], nrm[:, 0:R]).astype(bf16)
        pg = nn(wo[pl.ds(160 * half, 160), :], gyt[:, 0:R]).astype(bf16)
        for b in range(3):
            dst[b, 0:480, :] = pa[:, 128 * b : 128 * b + 128]
            dst[b, 480:640, :] = pg[:, 128 * b : 128 * b + 128]

    project(1, psend)
    pl.semaphore_wait(barrier, len(greet))
    edge = 2 * c
    lane320 = lax.broadcasted_iota(jnp.int32, (320, 128), 1) < 64

    def pack_halo(k, block):
        top, low = block[0:320].astype(f32), block[320:640].astype(f32)
        first = jnp.where(lane320, top, pltpu.roll(low, 64, 1))
        last = jnp.where(lane320, pltpu.roll(top, 64, 1), low)
        hsend[k] = jnp.where(c == 0, first, last).astype(bf16)

    pack_halo(1, psend[edge])
    send("halo1", hsend.at[1], halo.at[c], chip(2 * c - 1, 1 - c))
    send("proj", psend, proj.at[pl.ds(3, 3)], peer)
    project(0, proj)
    pack_halo(0, proj[edge])
    send("halo0", hsend.at[0], halo.at[c], chip(2 * c - 1, c))
    send("gyt", gyt.at[:, pl.ds(0, R)], gyt.at[:, pl.ds(R, R)], peer)
    send("nt", nrm.at[:, pl.ds(0, R)], nrm.at[:, pl.ds(R, R)], peer)
    for s in range(3):
        idr[pl.ds(s, 1), :] = ids[pl.ds(6 * q + 3 * c + s, 1), :]
        idr[pl.ds(3 + s, 1), :] = ids[pl.ds(6 * q + 3 - 3 * c + s, 1), :]
    lane1 = lax.broadcasted_iota(jnp.int32, (1, 128), 1) < 64
    after = ids[pl.ds(lax.rem(6 * q + 6, 192), 1), :]
    before = ids[pl.ds(lax.rem(6 * q + 191, 192), 1), :]
    idr[pl.ds(6, 1), :] = jnp.where(lane1, after, before)
    for s in range(7):
        idc[s] = jnp.broadcast_to(idr[pl.ds(s, 1), :], (128, 128)).T

    wn[...] = wt[...].T

    def natural(s):
        kn[s] = proj[s, 160:320, :].T
        vn[s] = proj[s, 320:480, :].T

    for s in range(3):
        natural(s)
    arrived("proj")
    for s in range(3, 6):
        natural(s)

    pick = lambda a, b: jnp.where(c == 0, a, b) if a != b else a
    nxt = [pick(*p) for p in ((1, 1), (2, 2), (3, 6), (4, 4), (5, 5), (6, 0), (0, 3))]
    prv = [pick(*p) for p in ((6, 5), (0, 0), (1, 1), (2, 6), (3, 3), (4, 4), (5, 2))]
    lane160 = lax.broadcasted_iota(jnp.int32, (160, 128), 1) < 64
    zero = jnp.zeros((HD, 128), bf16)

    def diagonal(t):
        return jnp.concatenate(
            [jnp.concatenate([t[0:80], zero], axis=1), jnp.concatenate([zero, t[80:160]], axis=1)], axis=0
        )

    def diag_of(t):
        return jnp.concatenate([t[0:80, 0:128], t[80:160, 128:256]], axis=0)

    def lanes_of(s):
        return pl.ds(pl.multiple_of(128 * s, 128), 128)

    def keys_t(s, n, p, w):
        rest = jnp.where(lane160, proj[n, w : w + 160, :].astype(f32), proj[p, w : w + 160, :].astype(f32))
        return jnp.concatenate([proj[s, w : w + 160, :], rest.astype(bf16)], axis=1)

    def keys_n(t, s, n, p):
        return jnp.concatenate([t[s], t[n, 0:64], t[p, 64:128]], axis=0)

    def forward(s, n, p, inside=True):
        q2, g2 = diagonal(proj[s, 0:160, :]), diagonal(proj[s, 480:640, :])
        same = keys_n(idc, s, n, p) == idr[pl.ds(s, 1), :]
        same = jnp.concatenate([same, same], axis=1)
        scores = jnp.where(same, nn(keys_n(kn, s, n, p), q2) * SCALE, NEG)
        e = jnp.exp(scores - jnp.max(scores, axis=0, keepdims=True))
        w = e * (1.0 / jnp.sum(e, axis=0, keepdims=True))
        wts[s] = w
        probs = w.astype(bf16)
        att = diag_of(nn(keys_t(s, n, p, 320), probs)).astype(bf16)
        both = att.astype(f32) * proj[s, 480:640, :].astype(f32)
        delta[pl.ds(s, 1), :] = jnp.concatenate(
            [jnp.sum(both[0:80], axis=0, keepdims=True), jnp.sum(both[80:160], axis=0, keepdims=True)], axis=1
        )
        if inside:
            at[:, lanes_of(s)] = att
        gv = nt(g2, probs)
        main[s, 160:320, :] = gv[:, 0:128]
        sec[s, 160:320, :] = gv[:, 128:256]

    def backward(s, n, p, inside=True):
        q2, g2 = diagonal(proj[s, 0:160, :]), diagonal(proj[s, 480:640, :])
        ds = (wts[s] * (nn(keys_n(vn, s, n, p), g2) - delta[pl.ds(s, 1), :]) * SCALE).astype(bf16)
        if inside:
            gt[0:160, lanes_of(s)] = diag_of(nn(keys_t(s, n, p, 160), ds)).astype(bf16)
        gk = nt(q2, ds)
        main[s, 0:160, :] = gk[:, 0:128]
        sec[s, 0:160, :] = gk[:, 128:256]

    def combine(rows, to):
        for s in range(6):
            total = main[s, rows, :] + jnp.where(lane160, sec[prv[s], rows, :], sec[nxt[s], rows, :])
            gt[to : to + 160, 128 * s : 128 * s + 128] = total.astype(bf16)

    inner = [(1, 2, 0), (pick(2, 0), pick(3, 1), pick(1, 5)), (pick(3, 5), pick(4, 0), pick(2, 4)), (4, 5, 3)]
    outer = [(pick(0, 2), pick(1, 6), pick(6, 1)), (pick(5, 3), pick(6, 4), pick(4, 6)), (6, nxt[6], prv[6], False)]
    for block in inner:
        forward(*block)
    for block in inner:
        backward(*block)

    arrived("halo0")
    arrived("halo1")
    ha, hb = halo[0].astype(f32), halo[1].astype(f32)
    proj[6, 0:320, :] = jnp.where(lane320, ha, pltpu.roll(hb, 64, 1)).astype(bf16)
    proj[6, 320:640, :] = jnp.where(lane320, pltpu.roll(ha, 64, 1), hb).astype(bf16)
    natural(6)
    for block in outer:
        forward(*block)
    combine(slice(160, 320), 320)

    def z_start():
        for w, way in enumerate(WAYS):
            send(f"za{w}", pz.at[lax.rem(z + 8 + 3 * way, 8)], za.at[w], zdev(way))
        for w, way in enumerate(WAYS):
            send(f"zh{w}", pz.at[lax.rem(z + 4, 8), pl.ds(80 * w, 80)], zh.at[w], zdev(2 * way))
        for w, way in enumerate(WAYS):
            send(f"zn{w}", pz.at[lax.rem(z + 8 + way, 8)], zn.at[w], zdev(way))

    def z_pass():
        for w, way in enumerate(WAYS):
            arrived(f"za{w}")
            arrived(f"zh{w}")
            chunk = lax.rem(z + 8 + 2 * way, 8)
            for k in range(2):
                rows = pl.ds(80 * k, 80)
                total = pz[chunk, rows].astype(f32) + za[w, rows].astype(f32)
                if k == w:
                    total = total + zh[w].astype(f32)
                pz[chunk, rows] = total.astype(bf16)
            send(f"zb{w}", pz.at[chunk], zb.at[w], zdev(2 * way))

    def z_end():
        total = pz[z].astype(f32)
        for w in range(2):
            arrived(f"zn{w}")
            arrived(f"zb{w}")
            total = total + zn[w].astype(f32) + zb[w].astype(f32)
        for i in range(4):
            piece = total[40 * i : 40 * i + 40]
            acc[i] = piece
            xs[i] = jnp.concatenate([piece, jnp.zeros((8, WZ), f32)], axis=0).astype(bf16)
        for d in (2, 1, 3):
            send(f"xs{d}", xs.at[lax.rem(x + d, 4)], xr.at[d - 1], xdev(d))

    def x_start(t):
        for w, way in enumerate(WAYS):
            send(f"xa{t}{w}", px.at[t, lax.rem(x + 2, 4), pl.ds(160 * w, 160)], xa.at[t, w], xdev(way))

    def x_pass(t):
        for w, way in enumerate(WAYS):
            arrived(f"xa{t}{w}")
            chunk, rows = lax.rem(x + 4 + way, 4), pl.ds(160 * w, 160)
            px[t, chunk, rows] = (px[t, chunk, rows].astype(f32) + xa[t, w].astype(f32)).astype(bf16)
            send(f"xb{t}{w}", px.at[t, chunk], xb.at[t, w], xdev(way))

    def x_sum(t):
        arrived(f"xb{t}0")
        arrived(f"xb{t}1")
        total = px[t, x].astype(f32) + xb[t, 0].astype(f32) + xb[t, 1].astype(f32)
        for i in range(8):
            piece = total[40 * i : 40 * i + 40]
            accx[t, i] = piece
            zs[t, i] = jnp.concatenate([piece, jnp.zeros((8, 128), f32)], axis=0).astype(bf16)
        for d in (4, 3, 5, 2, 6, 1, 7):
            send(f"z{t}{d}", zs.at[t, lax.rem(z + d, 8)], zr.at[t, d - 1], zdev(d))

    def z_sum(t):
        total = accx[t, z]
        for d in range(1, 8):
            arrived(f"z{t}{d}")
            total = total + zr[t, d - 1].astype(f32)[0:40]
        return total

    arrived("gyt")
    arrived("nt")
    cols = jnp.concatenate([nt(gyt[...], at[...]), nt(nrm[...], gt[320:480, :])], axis=1)

    def by_owner(cols, i):
        rows = [cols[160 * j + 40 * i : 160 * j + 40 * i + 40] for j in range(8)]
        return jnp.concatenate(rows, axis=0).astype(bf16)

    for i in range(4):
        rows = by_owner(cols, i)
        px[0, i] = rows[:, 0:128]
        px[1, i] = rows[:, 128:256]
        px[2, i, :, 0:64] = rows[:, 256:320]
    x_start(0)
    x_start(1)

    for block in outer:
        backward(*block)
    combine(slice(0, 160), 160)
    send("gt", gt.at[:, pl.ds(R, R)], gtr, peer)
    first_z = nt(nrm[...], gt[0:WZ, :]).astype(bf16)
    for i in range(8):
        pz[i] = first_z[160 * i : 160 * i + 160]
    z_start()
    cols = nt(nrm[...], gt[WZ:320, :])
    for i in range(4):
        rows = by_owner(cols, i)
        px[2, i, :, 64:128] = rows[:, 0:64]
        px[3, i] = rows[:, 64:192]
    x_start(2)
    x_start(3)

    arrived("gt")
    ssum = jnp.zeros((1, R), f32)
    ones = jnp.ones((8, 128), bf16)
    for d in (2, 1, 3, 0):
        to = lax.rem(h + d, 4)
        rows = pl.ds(pl.multiple_of(320 * to, 64), 320)
        g = nn(wn[rows, 0:480], gt[:, 0:R]) + nn(wn[rows, 480:960], gtr[...])
        if d:
            ysend[d - 1] = g.astype(bf16)
            send(f"y{d}", ysend.at[d - 1], yrecv.at[d - 1], ydev(d))
        else:
            gnf[...] = g
        if d == 1:
            x_pass(0)
        if d == 3:
            x_pass(1)
        parts = []
        gains = jnp.zeros((320, 128), f32)
        for b in range(3):
            lanes = slice(128 * b, 128 * b + 128)
            gb = g[:, lanes] * xt[rows, lanes].astype(f32)
            parts.append(jnp.sum(gb * gcol[rows, :], axis=0, keepdims=True))
            gains = gains + gb * inv[:, lanes]
        ssum = ssum + jnp.concatenate(parts, axis=1)
        high = gains.astype(bf16)
        low = (gains - high.astype(f32)).astype(bf16)
        gp[pl.ds(to, 1), :] = (nt(ones, high) + nt(ones, low))[0:1]
    ssend[...] = jnp.broadcast_to(ssum, (8, R))
    for d in range(1, 4):
        send(f"s{d}", ssend, srecv.at[d - 1], ydev(d))
    for d in (4, 3, 5, 2, 6, 1, 7):
        send(f"gz{d}", gp, gzr.at[d - 1], zdev(d))
    x_pass(2)
    x_pass(3)
    z_pass()
    x_sum(0)
    x_sum(1)
    total = gp[...]
    for d in range(1, 8):
        arrived(f"gz{d}")
        total = total + gzr[d - 1]
    gzs[...] = total
    for d in range(1, 4):
        send(f"gx{d}", gzs, gxr.at[d - 1], xdev(d))
    x_sum(2)
    x_sum(3)
    total = gzs[...]
    for d in range(1, 4):
        arrived(f"gx{d}")
        total = total + gxr[d - 1]
    gcs[...] = total
    send("gcore", gcs, gcr, peer)
    z_end()
    arrived("gcore")
    gys[...] = gcs[...] + gcr[...]
    for d in range(1, 4):
        send(f"gy{d}", gys, gyr.at[d - 1], ydev(d))

    mine = pl.ds(pl.multiple_of(320 * h, 64), 320)
    gn = gnf[...]
    sums = ssum
    for d in range(1, 4):
        arrived(f"y{d}")
        arrived(f"s{d}")
        gn = gn + yrecv[d - 1].astype(f32)
        sums = sums + srecv[d - 1, 0:1, :]
    iv = inv[...]
    gc = jnp.concatenate([gcol[mine, :]] * 3, axis=1)
    xi = xt[mine, :].astype(f32) * iv
    gx = gyt[mine, 0:R].astype(f32) + iv * (gn * gc - xi * (iv * (sums * (1.0 / D))))
    gx_out[...] = gx.astype(bf16)

    parts = [None] + [z_sum(t) for t in range(TILES)]
    total = acc[x]
    for d in range(1, 4):
        arrived(f"xs{d}")
        total = total + xr[d - 1].astype(f32)[0:40]
    parts[0] = total
    both = jnp.concatenate(parts, axis=1)
    low, high = both[0:20], both[20:40]
    first = c == 0
    csend[0:20, :] = jnp.where(first, high, low)
    csend[20:24, :] = jnp.zeros((4, 640), f32)
    send("core", csend, crecv, peer)
    own = jnp.where(first, low, high)
    total = gys[pl.ds(h, 1), :]
    for d in range(1, 4):
        arrived(f"gy{d}")
        total = total + gyr[d - 1, pl.ds(h, 1), :]
    ggain_out[...] = total[0]
    arrived("core")
    other = crecv[0:20, :]
    sides = (jnp.where(first, own, other), jnp.where(first, other, own))
    for i, side in enumerate(sides):
        cols = slice(160 * i, 160 * i + 160)
        gqkv_out[0, :, cols] = jnp.concatenate([side[:, 0:128], side[:, 448:480]], axis=1)
        gqkv_out[1, :, cols] = side[:, 480:640]
        gqkv_out[2, :, cols] = side[:, 288:448]
        gout_out[:, cols] = side[:, 128:288]
    for cp in copies.values():
        cp.wait_send()


def hand_over(*refs):
    for src, dst in zip(refs[:4], refs[4:]):
        dst[...] = src[...]


def per_device(patches, norm_gain, w_qkv, w_out, grad_y, window_ids):
    wt = jnp.transpose(w_qkv, (1, 2, 0)).reshape(960, D)
    wo = jnp.transpose(w_out)
    V = pltpu.VMEM
    scratch = [
        V((R, D), bf16), V((R, D), bf16), V((960, D), bf16), V((320, D), bf16),
        V((192, 128), jnp.int32), V((10, 128), f32),
        V((D, R), bf16), V((D, 2 * R), bf16), V((D, 2 * R), bf16), V((D, 960), bf16),
        V((D, 128), f32), V((1, R), f32),
        V((3, 640, 128), bf16), V((7, 640, 128), bf16), V((2, 320, 128), bf16), V((2, 320, 128), bf16),
        V((7, 128, 160), bf16), V((7, 128, 160), bf16),
        V((8, 128), jnp.int32), V((7, 128, 128), jnp.int32),
        V((7, 320, 128), f32), V((7, 320, 128), f32),
        V((7, 256, 256), f32), V((8, 256), f32),
        V((480, 2 * R), bf16), V((160, 2 * R), bf16), V((480, R), bf16),
        V((8, 160, WZ), bf16), V((2, 160, WZ), bf16), V((2, 80, WZ), bf16),
        V((2, 160, WZ), bf16), V((2, 160, WZ), bf16),
        V((4, 40, WZ), f32), V((4, 48, WZ), bf16), V((3, 48, WZ), bf16),
        V((TILES, 4, 320, 128), bf16), V((TILES, 2, 160, 128), bf16),
        V((TILES, 2, 320, 128), bf16),
        V((TILES, 8, 40, 128), f32), V((TILES, 8, 48, 128), bf16), V((TILES, 7, 48, 128), bf16),
        V((24, 640), f32), V((24, 640), f32),
        V((320, R), f32), V((3, 320, R), bf16), V((3, 320, R), bf16),
        V((8, R), f32), V((3, 8, R), f32),
        V((4, 320), f32), V((3, 4, 320), f32), V((4, 320), f32), V((4, 320), f32),
        V((4, 320), f32), V((7, 4, 320), f32), V((4, 320), f32), V((3, 4, 320), f32),
        pltpu.SemaphoreType.DMA((12,)),
        pltpu.SemaphoreType.DMA((len(NAMES),)),
        pltpu.SemaphoreType.DMA((len(NAMES),)),
    ]
    results = pl.pallas_call(
        kernel,
        out_shape=(
            jax.ShapeDtypeStruct((320, R), bf16),
            jax.ShapeDtypeStruct((3, 20, 320), f32),
            jax.ShapeDtypeStruct((20, 320), f32),
            jax.ShapeDtypeStruct((320,), f32),
        ),
        in_specs=[pl.BlockSpec(memory_space=pl.ANY)] * 6,
        out_specs=[pl.BlockSpec(memory_space=pltpu.VMEM)] * 4,
        scratch_shapes=scratch,
        compiler_params=pltpu.CompilerParams(
            collective_id=0, has_side_effects=True, vmem_limit_bytes=56 * 1024 * 1024
        ),
    )(patches, grad_y, wt, wo, window_ids.reshape(192, 128), norm_gain.reshape(10, 128))
    vmem = pl.BlockSpec(memory_space=pltpu.VMEM)
    gx, gqkv, gout, ggain = pl.pallas_call(
        hand_over,
        out_shape=tuple(jax.ShapeDtypeStruct(r.shape, r.dtype) for r in results),
        in_specs=[vmem] * 4,
        out_specs=[vmem] * 4,
    )(*results)
    return gx.T, jnp.transpose(gqkv, (1, 0, 2)), gout, ggain


def solution(mesh):
    in_specs = (P("vis", None), P(), P(None, None, "head"), P(None, "head"), P("vis", None), P())
    out_specs = (P("vis", "head"), P("vis", None, "head"), P("vis", "head"), P("head"))
    return jax.shard_map(
        per_device, mesh=mesh, in_specs=in_specs, out_specs=out_specs, check_vma=False
    )
```

```python
import functools

import jax
import jax.numpy as jnp
from jax import lax
from jax.experimental import pallas as pl
from jax.experimental.pallas import tpu as pltpu
from jax.sharding import PartitionSpec as P

f32 = jnp.float32
bf16 = jnp.bfloat16
D = 1280
HD = 80
R = 384
SCALE = HD ** (-0.5)
EPS = 1e-06
MESH = pl.DeviceIdType.MESH
NEG = -1e30
WZ = 128
WX = 512
TILES = WX // 128
WAYS = (1, -1)


def nn(a, b):
    return lax.dot_general(a, b, (((1,), (0,)), ((), ())), preferred_element_type=f32)


def nt(a, b, precision=None):
    return lax.dot_general(
        a, b, (((1,), (1,)), ((), ())), preferred_element_type=f32, precision=precision
    )


NAMES = ["proj", "halo0", "halo1", "nt", "gyt", "gt", "core", "gcore"]
NAMES += [f"z{n}{w}" for n in "ahnb" for w in range(2)]
NAMES += [f"xs{d}" for d in range(1, 4)]
NAMES += [f"x{n}{t}{w}" for n in "ab" for t in range(TILES) for w in range(2)]
NAMES += [f"z{t}{d}" for t in range(TILES) for d in range(1, 8)]
NAMES += [f"{n}{d}" for n in ("y", "s", "gx", "gy") for d in range(1, 4)]
NAMES += [f"gz{d}" for d in range(1, 8)]
MSG = {name: i for i, name in enumerate(NAMES)}


def kernel(
    x_hbm, gy_hbm, wt_hbm, wo_hbm, ids_hbm, gain_hbm,
    gx_out, gqkv_out, gout_out, ggain_out,
    x_v, gy_v, wt, wo, ids, gain,
    xt, nrm, gyt, wn, gcol, inv,
    psend, proj, hsend, halo, kn, vn, idr, idc, main, sec, wts, delta,
    gt, at, gtr,
    pz, za, zh, zn, zb, acc, xs, xr,
    px, xa, xb, accx, zs, zr, csend, crecv,
    gnf, ysend, yrecv, ssend, srecv,
    gp, gxr, gcs, gcr, gzs, gzr, gys, gyr,
    lsem, send_sem, recv_sem,
):
    v = lax.axis_index("vis")
    h = lax.axis_index("head")
    c = lax.rem(v, 2)
    q = v // 2
    x = lax.rem(q, 4)
    z = v // 8
    dev = lambda zz, xx, cc: (zz * 8 + xx * 2 + cc, h)
    zdev = lambda d: dev(lax.rem(z + d + 8, 8), x, c)
    xdev = lambda d: dev(z, lax.rem(x + d + 4, 4), c)
    ydev = lambda d: (v, lax.rem(h + d, 4))
    peer = (v + 1 - 2 * c, h)
    chip = lambda d, cc: (2 * lax.rem(q + d + 32, 32) + cc, h)

    loads = []

    def load(src, dst):
        cp = pltpu.make_async_copy(src, dst, lsem.at[len(loads)])
        cp.start()
        loads.append(cp)
        return cp

    ld_x = load(x_hbm, x_v)
    ld_gain = load(gain_hbm, gain)
    ld_gy = load(gy_hbm, gy_v)
    ld_w = []
    for k in (1, 0):
        half = c if k == 0 else 1 - c
        for comp in range(3):
            src = pl.multiple_of(320 * comp + 160 * half, 16)
            ld_w.append(load(wt_hbm.at[pl.ds(src, 160), :], wt.at[pl.ds(480 * k + 160 * comp, 160), :]))
        src = pl.multiple_of(160 * half, 16)
        ld_w.append(load(wo_hbm.at[pl.ds(src, 160), :], wo.at[pl.ds(160 * k, 160), :]))
    ld_ids = load(ids_hbm, ids)

    barrier = pltpu.get_barrier_semaphore()
    greet = [peer]
    greet += [zdev(d) for d in range(1, 8)]
    greet += [xdev(d) for d in range(1, 4)]
    greet += [ydev(d) for d in range(1, 4)]
    greet += [chip(2 * c - 1, 0), chip(2 * c - 1, 1), chip(1 - 2 * c, c)]
    for d in greet:
        pl.semaphore_signal(barrier, inc=1, device_id=d, device_id_type=MESH)

    copies = {}

    def send(name, src, dst, to):
        i = MSG[name]
        cp = pltpu.make_async_remote_copy(
            src_ref=src, dst_ref=dst, send_sem=send_sem.at[i], recv_sem=recv_sem.at[i],
            device_id=to, device_id_type=MESH,
        )
        cp.start()
        copies[name] = cp

    def arrived(name):
        copies[name].wait_recv()
    ld_x.wait()
    ld_gain.wait()
    xt[...] = x_v[...].T
    for i in range(10):
        gcol[pl.ds(128 * i, 128), :] = jnp.broadcast_to(gain[pl.ds(i, 1), :], (128, 128)).T
    for b in range(3):
        lanes = pl.ds(128 * b, 128)
        xf = xt[:, lanes].astype(f32)
        iv = lax.rsqrt(jnp.sum(xf * xf, axis=0, keepdims=True) * (1.0 / D) + EPS)
        inv[:, lanes] = iv
        nrm[:, lanes] = (xf * iv * gcol[...]).astype(bf16)
    ld_gy.wait()
    gyt[:, 0:R] = gy_v[...].T
    for cp in ld_w:
        cp.wait()
    ld_ids.wait()
    def project(half, dst):
        pa = nn(wt[pl.ds(480 * half, 480), :], nrm[:, 0:R]).astype(bf16)
        pg = nn(wo[pl.ds(160 * half, 160), :], gyt[:, 0:R]).astype(bf16)
        for b in range(3):
            dst[b, 0:480, :] = pa[:, 128 * b : 128 * b + 128]
            dst[b, 480:640, :] = pg[:, 128 * b : 128 * b + 128]

    project(1, psend)
    pl.semaphore_wait(barrier, len(greet))
    edge = 2 * c
    lane320 = lax.broadcasted_iota(jnp.int32, (320, 128), 1) < 64

    def pack_halo(k, block):
        top, low = block[0:320].astype(f32), block[320:640].astype(f32)
        first = jnp.where(lane320, top, pltpu.roll(low, 64, 1))
        last = jnp.where(lane320, pltpu.roll(top, 64, 1), low)
        hsend[k] = jnp.where(c == 0, first, last).astype(bf16)

    pack_halo(1, psend[edge])
    send("halo1", hsend.at[1], halo.at[c], chip(2 * c - 1, 1 - c))
    send("proj", psend, proj.at[pl.ds(3, 3)], peer)
    project(0, proj)
    pack_halo(0, proj[edge])
    send("halo0", hsend.at[0], halo.at[c], chip(2 * c - 1, c))
    send("gyt", gyt.at[:, pl.ds(0, R)], gyt.at[:, pl.ds(R, R)], peer)
    send("nt", nrm.at[:, pl.ds(0, R)], nrm.at[:, pl.ds(R, R)], peer)
    for s in range(3):
        idr[pl.ds(s, 1), :] = ids[pl.ds(6 * q + 3 * c + s, 1), :]
        idr[pl.ds(3 + s, 1), :] = ids[pl.ds(6 * q + 3 - 3 * c + s, 1), :]
    lane1 = lax.broadcasted_iota(jnp.int32, (1, 128), 1) < 64
    after = ids[pl.ds(lax.rem(6 * q + 6, 192), 1), :]
    before = ids[pl.ds(lax.rem(6 * q + 191, 192), 1), :]
    idr[pl.ds(6, 1), :] = jnp.where(lane1, after, before)
    for s in range(7):
        idc[s] = jnp.broadcast_to(idr[pl.ds(s, 1), :], (128, 128)).T

    wn[...] = wt[...].T

    def natural(s):
        kn[s] = proj[s, 160:320, :].T
        vn[s] = proj[s, 320:480, :].T

    for s in range(3):
        natural(s)
    arrived("proj")
    for s in range(3, 6):
        natural(s)

    pick = lambda a, b: jnp.where(c == 0, a, b) if a != b else a
    nxt = [pick(*p) for p in ((1, 1), (2, 2), (3, 6), (4, 4), (5, 5), (6, 0), (0, 3))]
    prv = [pick(*p) for p in ((6, 5), (0, 0), (1, 1), (2, 6), (3, 3), (4, 4), (5, 2))]
    lane160 = lax.broadcasted_iota(jnp.int32, (160, 128), 1) < 64
    zero = jnp.zeros((HD, 128), bf16)

    def diagonal(t):
        return jnp.concatenate(
            [jnp.concatenate([t[0:80], zero], axis=1), jnp.concatenate([zero, t[80:160]], axis=1)], axis=0
        )

    def diag_of(t):
        return jnp.concatenate([t[0:80, 0:128], t[80:160, 128:256]], axis=0)

    def lanes_of(s):
        return pl.ds(pl.multiple_of(128 * s, 128), 128)

    def keys_t(s, n, p, w):
        rest = jnp.where(lane160, proj[n, w : w + 160, :].astype(f32), proj[p, w : w + 160, :].astype(f32))
        return jnp.concatenate([proj[s, w : w + 160, :], rest.astype(bf16)], axis=1)

    def keys_n(t, s, n, p):
        return jnp.concatenate([t[s], t[n, 0:64], t[p, 64:128]], axis=0)

    def forward(s, n, p, inside=True):
        q2, g2 = diagonal(proj[s, 0:160, :]), diagonal(proj[s, 480:640, :])
        same = keys_n(idc, s, n, p) == idr[pl.ds(s, 1), :]
        same = jnp.concatenate([same, same], axis=1)
        scores = jnp.where(same, nn(keys_n(kn, s, n, p), q2) * SCALE, NEG)
        e = jnp.exp(scores - jnp.max(scores, axis=0, keepdims=True))
        w = e * (1.0 / jnp.sum(e, axis=0, keepdims=True))
        wts[s] = w
        probs = w.astype(bf16)
        att = diag_of(nn(keys_t(s, n, p, 320), probs)).astype(bf16)
        both = att.astype(f32) * proj[s, 480:640, :].astype(f32)
        delta[pl.ds(s, 1), :] = jnp.concatenate(
            [jnp.sum(both[0:80], axis=0, keepdims=True), jnp.sum(both[80:160], axis=0, keepdims=True)], axis=1
        )
        if inside:
            at[:, lanes_of(s)] = att
        gv = nt(g2, probs)
        main[s, 160:320, :] = gv[:, 0:128]
        sec[s, 160:320, :] = gv[:, 128:256]

    def backward(s, n, p, inside=True):
        q2, g2 = diagonal(proj[s, 0:160, :]), diagonal(proj[s, 480:640, :])
        ds = (wts[s] * (nn(keys_n(vn, s, n, p), g2) - delta[pl.ds(s, 1), :]) * SCALE).astype(bf16)
        if inside:
            gt[0:160, lanes_of(s)] = diag_of(nn(keys_t(s, n, p, 160), ds)).astype(bf16)
        gk = nt(q2, ds)
        main[s, 0:160, :] = gk[:, 0:128]
        sec[s, 0:160, :] = gk[:, 128:256]

    def combine(rows, to):
        for s in range(6):
            total = main[s, rows, :] + jnp.where(lane160, sec[prv[s], rows, :], sec[nxt[s], rows, :])
            gt[to : to + 160, 128 * s : 128 * s + 128] = total.astype(bf16)

    inner = [(1, 2, 0), (pick(2, 0), pick(3, 1), pick(1, 5)), (pick(3, 5), pick(4, 0), pick(2, 4)), (4, 5, 3)]
    outer = [(pick(0, 2), pick(1, 6), pick(6, 1)), (pick(5, 3), pick(6, 4), pick(4, 6)), (6, nxt[6], prv[6], False)]
    for block in inner:
        forward(*block)
    for block in inner:
        backward(*block)

    arrived("halo0")
    arrived("halo1")
    ha, hb = halo[0].astype(f32), halo[1].astype(f32)
    proj[6, 0:320, :] = jnp.where(lane320, ha, pltpu.roll(hb, 64, 1)).astype(bf16)
    proj[6, 320:640, :] = jnp.where(lane320, pltpu.roll(ha, 64, 1), hb).astype(bf16)
    natural(6)
    for block in outer:
        forward(*block)
    combine(slice(160, 320), 320)

    def z_start():
        for w, way in enumerate(WAYS):
            send(f"za{w}", pz.at[lax.rem(z + 8 + 3 * way, 8)], za.at[w], zdev(way))
        for w, way in enumerate(WAYS):
            send(f"zh{w}", pz.at[lax.rem(z + 4, 8), pl.ds(80 * w, 80)], zh.at[w], zdev(2 * way))
        for w, way in enumerate(WAYS):
            send(f"zn{w}", pz.at[lax.rem(z + 8 + way, 8)], zn.at[w], zdev(way))

    def z_pass():
        for w, way in enumerate(WAYS):
            arrived(f"za{w}")
            arrived(f"zh{w}")
            chunk = lax.rem(z + 8 + 2 * way, 8)
            for k in range(2):
                rows = pl.ds(80 * k, 80)
                total = pz[chunk, rows].astype(f32) + za[w, rows].astype(f32)
                if k == w:
                    total = total + zh[w].astype(f32)
                pz[chunk, rows] = total.astype(bf16)
            send(f"zb{w}", pz.at[chunk], zb.at[w], zdev(2 * way))

    def z_end():
        total = pz[z].astype(f32)
        for w in range(2):
            arrived(f"zn{w}")
            arrived(f"zb{w}")
            total = total + zn[w].astype(f32) + zb[w].astype(f32)
        for i in range(4):
            piece = total[40 * i : 40 * i + 40]
            acc[i] = piece
            xs[i] = jnp.concatenate([piece, jnp.zeros((8, WZ), f32)], axis=0).astype(bf16)
        for d in (2, 1, 3):
            send(f"xs{d}", xs.at[lax.rem(x + d, 4)], xr.at[d - 1], xdev(d))

    def x_start(t):
        for w, way in enumerate(WAYS):
            send(f"xa{t}{w}", px.at[t, lax.rem(x + 2, 4), pl.ds(160 * w, 160)], xa.at[t, w], xdev(way))

    def x_pass(t):
        for w, way in enumerate(WAYS):
            arrived(f"xa{t}{w}")
            chunk, rows = lax.rem(x + 4 + way, 4), pl.ds(160 * w, 160)
            px[t, chunk, rows] = (px[t, chunk, rows].astype(f32) + xa[t, w].astype(f32)).astype(bf16)
            send(f"xb{t}{w}", px.at[t, chunk], xb.at[t, w], xdev(way))

    def x_sum(t):
        arrived(f"xb{t}0")
        arrived(f"xb{t}1")
        total = px[t, x].astype(f32) + xb[t, 0].astype(f32) + xb[t, 1].astype(f32)
        for i in range(8):
            piece = total[40 * i : 40 * i + 40]
            accx[t, i] = piece
            zs[t, i] = jnp.concatenate([piece, jnp.zeros((8, 128), f32)], axis=0).astype(bf16)
        for d in (4, 3, 5, 2, 6, 1, 7):
            send(f"z{t}{d}", zs.at[t, lax.rem(z + d, 8)], zr.at[t, d - 1], zdev(d))

    def z_sum(t):
        total = accx[t, z]
        for d in range(1, 8):
            arrived(f"z{t}{d}")
            total = total + zr[t, d - 1].astype(f32)[0:40]
        return total

    arrived("gyt")
    arrived("nt")
    cols = jnp.concatenate([nt(gyt[...], at[...]), nt(nrm[...], gt[320:480, :])], axis=1)

    def by_owner(cols, i):
        rows = [cols[160 * j + 40 * i : 160 * j + 40 * i + 40] for j in range(8)]
        return jnp.concatenate(rows, axis=0).astype(bf16)

    for i in range(4):
        rows = by_owner(cols, i)
        px[0, i] = rows[:, 0:128]
        px[1, i] = rows[:, 128:256]
        px[2, i, :, 0:64] = rows[:, 256:320]
    x_start(0)
    x_start(1)

    for block in outer:
        backward(*block)
    combine(slice(0, 160), 160)
    send("gt", gt.at[:, pl.ds(R, R)], gtr, peer)
    first_z = nt(nrm[...], gt[0:WZ, :]).astype(bf16)
    for i in range(8):
        pz[i] = first_z[160 * i : 160 * i + 160]
    z_start()
    cols = nt(nrm[...], gt[WZ:320, :])
    for i in range(4):
        rows = by_owner(cols, i)
        px[2, i, :, 64:128] = rows[:, 0:64]
        px[3, i] = rows[:, 64:192]
    x_start(2)
    x_start(3)

    arrived("gt")
    ssum = jnp.zeros((1, R), f32)
    ones = jnp.ones((8, 128), bf16)
    for d in (2, 1, 3, 0):
        to = lax.rem(h + d, 4)
        rows = pl.ds(pl.multiple_of(320 * to, 64), 320)
        g = nn(wn[rows, 0:480], gt[:, 0:R]) + nn(wn[rows, 480:960], gtr[...])
        if d:
            ysend[d - 1] = g.astype(bf16)
            send(f"y{d}", ysend.at[d - 1], yrecv.at[d - 1], ydev(d))
        else:
            gnf[...] = g
        if d == 1:
            x_pass(0)
        if d == 3:
            x_pass(1)
        parts = []
        gains = jnp.zeros((320, 128), f32)
        for b in range(3):
            lanes = slice(128 * b, 128 * b + 128)
            gb = g[:, lanes] * xt[rows, lanes].astype(f32)
            parts.append(jnp.sum(gb * gcol[rows, :], axis=0, keepdims=True))
            gains = gains + gb * inv[:, lanes]
        ssum = ssum + jnp.concatenate(parts, axis=1)
        high = gains.astype(bf16)
        low = (gains - high.astype(f32)).astype(bf16)
        gp[pl.ds(to, 1), :] = (nt(ones, high) + nt(ones, low))[0:1]
    ssend[...] = jnp.broadcast_to(ssum, (8, R))
    for d in range(1, 4):
        send(f"s{d}", ssend, srecv.at[d - 1], ydev(d))
    for d in (4, 3, 5, 2, 6, 1, 7):
        send(f"gz{d}", gp, gzr.at[d - 1], zdev(d))
    x_pass(2)
    z_pass()
    x_pass(3)
    x_sum(0)
    x_sum(1)
    total = gp[...]
    for d in range(1, 8):
        arrived(f"gz{d}")
        total = total + gzr[d - 1]
    gzs[...] = total
    for d in range(1, 4):
        send(f"gx{d}", gzs, gxr.at[d - 1], xdev(d))
    x_sum(2)
    z_end()
    x_sum(3)
    total = gzs[...]
    for d in range(1, 4):
        arrived(f"gx{d}")
        total = total + gxr[d - 1]
    gcs[...] = total
    send("gcore", gcs, gcr, peer)
    arrived("gcore")
    gys[...] = gcs[...] + gcr[...]
    for d in range(1, 4):
        send(f"gy{d}", gys, gyr.at[d - 1], ydev(d))

    mine = pl.ds(pl.multiple_of(320 * h, 64), 320)
    gn = gnf[...]
    sums = ssum
    for d in range(1, 4):
        arrived(f"y{d}")
        arrived(f"s{d}")
        gn = gn + yrecv[d - 1].astype(f32)
        sums = sums + srecv[d - 1, 0:1, :]
    iv = inv[...]
    gc = jnp.concatenate([gcol[mine, :]] * 3, axis=1)
    xi = xt[mine, :].astype(f32) * iv
    gx = gyt[mine, 0:R].astype(f32) + iv * (gn * gc - xi * (iv * (sums * (1.0 / D))))
    gx_out[...] = gx.astype(bf16)

    parts = [None] + [z_sum(t) for t in range(TILES)]
    total = acc[x]
    for d in range(1, 4):
        arrived(f"xs{d}")
        total = total + xr[d - 1].astype(f32)[0:40]
    parts[0] = total
    both = jnp.concatenate(parts, axis=1)
    low, high = both[0:20], both[20:40]
    first = c == 0
    csend[0:20, :] = jnp.where(first, high, low)
    csend[20:24, :] = jnp.zeros((4, 640), f32)
    send("core", csend, crecv, peer)
    own = jnp.where(first, low, high)
    total = gys[pl.ds(h, 1), :]
    for d in range(1, 4):
        arrived(f"gy{d}")
        total = total + gyr[d - 1, pl.ds(h, 1), :]
    ggain_out[...] = total[0]
    arrived("core")
    other = crecv[0:20, :]
    sides = (jnp.where(first, own, other), jnp.where(first, other, own))
    for i, side in enumerate(sides):
        cols = slice(160 * i, 160 * i + 160)
        gqkv_out[0, :, cols] = jnp.concatenate([side[:, 0:128], side[:, 448:480]], axis=1)
        gqkv_out[1, :, cols] = side[:, 480:640]
        gqkv_out[2, :, cols] = side[:, 288:448]
        gout_out[:, cols] = side[:, 128:288]
    for cp in copies.values():
        cp.wait_send()


def hand_over(*refs):
    for src, dst in zip(refs[:4], refs[4:]):
        dst[...] = src[...]


def per_device(patches, norm_gain, w_qkv, w_out, grad_y, window_ids):
    wt = jnp.transpose(w_qkv, (1, 2, 0)).reshape(960, D)
    wo = jnp.transpose(w_out)
    V = pltpu.VMEM
    scratch = [
        V((R, D), bf16), V((R, D), bf16), V((960, D), bf16), V((320, D), bf16),
        V((192, 128), jnp.int32), V((10, 128), f32),
        V((D, R), bf16), V((D, 2 * R), bf16), V((D, 2 * R), bf16), V((D, 960), bf16),
        V((D, 128), f32), V((1, R), f32),
        V((3, 640, 128), bf16), V((7, 640, 128), bf16), V((2, 320, 128), bf16), V((2, 320, 128), bf16),
        V((7, 128, 160), bf16), V((7, 128, 160), bf16),
        V((8, 128), jnp.int32), V((7, 128, 128), jnp.int32),
        V((7, 320, 128), f32), V((7, 320, 128), f32),
        V((7, 256, 256), f32), V((8, 256), f32),
        V((480, 2 * R), bf16), V((160, 2 * R), bf16), V((480, R), bf16),
        V((8, 160, WZ), bf16), V((2, 160, WZ), bf16), V((2, 80, WZ), bf16),
        V((2, 160, WZ), bf16), V((2, 160, WZ), bf16),
        V((4, 40, WZ), f32), V((4, 48, WZ), bf16), V((3, 48, WZ), bf16),
        V((TILES, 4, 320, 128), bf16), V((TILES, 2, 160, 128), bf16),
        V((TILES, 2, 320, 128), bf16),
        V((TILES, 8, 40, 128), f32), V((TILES, 8, 48, 128), bf16), V((TILES, 7, 48, 128), bf16),
        V((24, 640), f32), V((24, 640), f32),
        V((320, R), f32), V((3, 320, R), bf16), V((3, 320, R), bf16),
        V((8, R), f32), V((3, 8, R), f32),
        V((4, 320), f32), V((3, 4, 320), f32), V((4, 320), f32), V((4, 320), f32),
        V((4, 320), f32), V((7, 4, 320), f32), V((4, 320), f32), V((3, 4, 320), f32),
        pltpu.SemaphoreType.DMA((12,)),
        pltpu.SemaphoreType.DMA((len(NAMES),)),
        pltpu.SemaphoreType.DMA((len(NAMES),)),
    ]
    results = pl.pallas_call(
        kernel,
        out_shape=(
            jax.ShapeDtypeStruct((320, R), bf16),
            jax.ShapeDtypeStruct((3, 20, 320), f32),
            jax.ShapeDtypeStruct((20, 320), f32),
            jax.ShapeDtypeStruct((320,), f32),
        ),
        in_specs=[pl.BlockSpec(memory_space=pl.ANY)] * 6,
        out_specs=[pl.BlockSpec(memory_space=pltpu.VMEM)] * 4,
        scratch_shapes=scratch,
        compiler_params=pltpu.CompilerParams(
            collective_id=0, has_side_effects=True, vmem_limit_bytes=56 * 1024 * 1024
        ),
    )(patches, grad_y, wt, wo, window_ids.reshape(192, 128), norm_gain.reshape(10, 128))
    vmem = pl.BlockSpec(memory_space=pltpu.VMEM)
    gx, gqkv, gout, ggain = pl.pallas_call(
        hand_over,
        out_shape=tuple(jax.ShapeDtypeStruct(r.shape, r.dtype) for r in results),
        in_specs=[vmem] * 4,
        out_specs=[vmem] * 4,
    )(*results)
    return gx.T, jnp.transpose(gqkv, (1, 0, 2)), gout, ggain


def solution(mesh):
    in_specs = (P("vis", None), P(), P(None, None, "head"), P(None, "head"), P("vis", None), P())
    out_specs = (P("vis", "head"), P("vis", None, "head"), P("vis", "head"), P("head"))
    return jax.shard_map(
        per_device, mesh=mesh, in_specs=in_specs, out_specs=out_specs, check_vma=False
    )
```
